32 devices in a mesh: grid: 16 (over z, x, core), mem: 2 (over y).
Axes of the slice: x: 2, y: 2, z: 4, core: 2. Of those that a mesh axis runs over, the one named last changes fastest.
Arguments:
- ens: bfloat16 [20, 4, 32, 16384], P('mem', None, None, 'grid'), may hold values from -6 to 6
- control: float32 [4, 32, 16384], P(None, None, 'grid'), may hold values from -6 to 6
- col_count: int32 [128], P('grid'), may hold values from 64 to 128, as said below
- level_index: int32 [32], replicated, may hold values from 43 to 136, as said below
- pair_blocks: int32 [1536, 2], P('grid'), may hold values from 0 to 127, as said below
- loc_blocks: bfloat16 [1536, 128, 128], P('grid'), may hold values from -0.109375 to 0.109375
Outputs:
- mixed: float32 [4, 32, 16384], P(None, None, ('grid', 'mem'))
The draws below stay inside these ranges and needn't reach their ends.
Inputs may be any that keep to these rules, and one draw needn't show every extreme that they name: `pair_blocks`: rows come in groups of 12, one group for each block b in order; group b holds the pairs (b, (b + k) mod 128) for k = 0, k = 12 and 10 further distinct k between 1 and 11. `col_count`: some block is full. `level_index`: strictly increasing by steps of 1 to 3; the last is 136.
All inputs are finite; a program needn't handle non-finite values.
Results may differ from the reference program's by a relative error of at most 0.0029.
Values may be sent and summed in bfloat16 or wider, within the bound.
A program may use at most 64 MiB of HBM per device.

```python
import jax
import jax.numpy as jnp
from jax import lax

BLOCK = 128
LEV = 32
SLOTS = 4
PER = 12
SPAN = 12
MEMBERS = 20
BLOCKS = 128
COLUMNS = 16384


def draw_col_count(key, part):
    key = jax.random.fold_in(key, 11)
    count_key, full_key = jax.random.split(key)
    counts = jax.random.randint(count_key, (BLOCKS,), BLOCK // 2, BLOCK + 1)
    full = jax.random.randint(full_key, (), 0, BLOCKS)
    return jnp.where(jnp.arange(BLOCKS) == full, BLOCK, counts).astype(jnp.int32)


def draw_level_index(key, part):
    key = jax.random.fold_in(key, 12)
    steps = jax.random.randint(key, (LEV,), 1, 4)
    tail = jnp.cumsum(steps[::-1])[::-1] - steps
    return (136 - tail).astype(jnp.int32)


def draw_pair_blocks(key, part):
    key = jax.random.fold_in(key, 13)
    block_keys = jax.random.split(key, BLOCKS)
    picked = jax.vmap(lambda k: jax.random.permutation(k, SPAN - 1)[:PER - 2] + 1)(block_keys)
    fixed = jnp.broadcast_to(jnp.array([0, SPAN], jnp.int32), (BLOCKS, 2))
    offsets = jnp.concatenate([fixed, picked.astype(jnp.int32)], axis=1)
    first = jnp.broadcast_to(jnp.arange(BLOCKS, dtype=jnp.int32)[:, None], (BLOCKS, PER))
    second = (first + offsets) % BLOCKS
    return jnp.stack([first, second], axis=-1).reshape(BLOCKS * PER, 2).astype(jnp.int32)


def steps_of(own_key, shape, cuts, low, largest):
    def one(axis_at, parts):
        heights = jax.random.uniform(jax.random.fold_in(jax.random.fold_in(own_key, 6), axis_at), (parts,), jnp.float32, low / len(cuts), largest / len(cuts))
        return jnp.repeat(jnp.exp(heights), shape[axis_at] // parts).reshape((-1,) + (1,) * (len(shape) - axis_at - 1))

    gain = one(*cuts[0])
    for cut in cuts[1:]:
        gain = gain * one(*cut)
    return gain


def centred(rng, extent, scale, reach, cuts=(), held_as=jnp.bfloat16):
    result = jax.random.normal(rng, extent, jnp.float32) * scale
    if len(cuts) > 0:
        result = steps_of(rng, extent, cuts, -0.22, 0.18) * result
    return jnp.clip(result, min=-reach, max=reach).astype(held_as)


def setup_inputs(seed: int = 0) -> dict:
    key_list = jax.random.split(jax.random.key(seed), 7)
    return {
        "ens": centred(key_list[0], (MEMBERS, SLOTS, LEV, COLUMNS), 1.0, 6.0, ((0, 2), (3, 16))),
        "control": centred(key_list[1], (SLOTS, LEV, COLUMNS), 1.0, 6.0, ((2, 16),), jnp.float32),
        "col_count": draw_col_count(jax.random.fold_in(key_list[6], 71), 0),
        "level_index": draw_level_index(jax.random.fold_in(key_list[6], 71), 0),
        "pair_blocks": draw_pair_blocks(jax.random.fold_in(key_list[6], 71), 0),
        "loc_blocks": centred(key_list[5], (BLOCKS * PER, BLOCK, BLOCK), (256 * PER) ** -0.5, 0.109375, ((0, 16),)),
    }


vertical_scale = 8.0


def reference(ens, control, col_count, level_index, pair_blocks, loc_blocks):
    columns = jnp.arange(BLOCKS * BLOCK)
    live = ((columns % BLOCK) < jnp.repeat(col_count, BLOCK)).astype(jnp.float32)
    masked = control * live
    levels = level_index.astype(jnp.float32)
    vert = jnp.exp(-jnp.abs(levels[:, None] - levels[None, :]) / vertical_scale)

    def one_member(member):
        weighted = jnp.sum(member.astype(jnp.float32) * masked, axis=0)
        return jnp.dot(vert, weighted, precision=lax.Precision.HIGHEST).astype(jnp.bfloat16)

    lifted = lax.map(one_member, ens)
    by_block = lifted.reshape(MEMBERS, LEV, BLOCKS, BLOCK).transpose(2, 0, 1, 3)
    pairs = pair_blocks.reshape(BLOCKS, PER, 2)
    locs = loc_blocks.reshape(BLOCKS, PER, BLOCK, BLOCK)

    def step(spread, item):
        group, local_loc = item
        first_rows = by_block[group[:, 0]].astype(jnp.float32)
        second_rows = by_block[group[:, 1]].astype(jnp.float32)
        loc_wide = local_loc.astype(jnp.float32)
        to_first = jnp.einsum("pab,pmlb->pmla", loc_wide, second_rows)
        apart = (group[:, 0] != group[:, 1]).astype(jnp.float32)
        to_second = jnp.einsum("pab,pmla->pmlb", loc_wide, first_rows) * apart[:, None, None, None]
        spread = spread.at[group[:, 0]].add(to_first)
        spread = spread.at[group[:, 1]].add(to_second)
        return spread, None

    start = jnp.zeros((BLOCKS, MEMBERS, LEV, BLOCK), jnp.float32)
    spread, unused = lax.scan(step, start, (pairs, locs))
    spread_cols = spread.transpose(1, 2, 0, 3).reshape(MEMBERS, LEV, BLOCKS * BLOCK)

    def add_member(total, item):
        member, member_spread = item
        return total + member.astype(jnp.float32) * member_spread[None], None

    total, unused = lax.scan(add_member, jnp.zeros((SLOTS, LEV, BLOCKS * BLOCK), jnp.float32), (ens, spread_cols))
    return total * live / (MEMBERS - 1)
```

```python
import functools

import jax
import jax.numpy as jnp
from jax import lax
from jax.experimental import pallas as pl
from jax.experimental.pallas import tpu as pltpu
from jax.sharding import PartitionSpec as P

SPAN = 12
MESH = pl.DeviceIdType.MESH


vertical_scale = 8.0


def kernel(
    sizes,
    count_ref,
    level_ref,
    slot_ref,
    ens_hbm,
    control_hbm,
    loc_hbm,
    out_ref,
    ens,
    control,
    loc,
    table,
    far,
    relay_in,
    near_in,
    spread,
    terms,
    terms_in,
    in_sems,
    lift_send,
    lift_recv,
    far_send,
    far_recv,
    term_send,
    term_recv,
):
    members, slots, levels, own, width, devices, peers = sizes
    rows = members * levels
    extra = SPAN - own
    pairs = loc_hbm.shape[0]
    here = lax.axis_index("grid")
    mem = lax.axis_index("mem")
    up = lax.rem(here + 1, devices)
    down = lax.rem(here + devices - 1, devices)

    def cols(first, last):
        return slice(first * width, last * width)

    step = 2 if own % 2 == 0 else 1
    parts = own // step
    loads = []
    for part in range(parts):
        at = cols(part * step, (part + 1) * step)
        a = pltpu.make_async_copy(
            control_hbm.at[:, :, at], control.at[:, :, at], in_sems.at[2 * part]
        )
        b = pltpu.make_async_copy(
            ens_hbm.at[:, :, :, at], ens.at[:, :, :, at], in_sems.at[2 * part + 1]
        )
        a.start()
        b.start()
        loads.append((a, b))
    load_loc = pltpu.make_async_copy(loc_hbm, loc.at[pl.ds(0, pairs)], in_sems.at[2 * parts])
    load_loc.start()

    barrier = pltpu.get_barrier_semaphore()
    for other in (up, down):
        pl.semaphore_signal(barrier, inc=1, device_id={"grid": other}, device_id_type=MESH)
    for away in range(1, peers):
        pl.semaphore_signal(
            barrier, inc=1, device_id={"mem": lax.rem(mem + away, peers)}, device_id_type=MESH
        )

    loc[pairs] = jnp.zeros((width, width), loc.dtype)

    group = max(g for g in range(1, members + 1) if members % g == 0 and g * levels <= 256)
    size = group * levels
    down_at = lax.broadcasted_iota(jnp.int32, (size, 1), 0)
    across_at = lax.broadcasted_iota(jnp.int32, (1, size), 1)
    level_down = jnp.zeros((size, 1), jnp.float32)
    level_across = jnp.zeros((1, size), jnp.float32)
    for l in range(levels):
        value = level_ref[l].astype(jnp.float32)
        level_down = jnp.where(down_at % levels == l, value, level_down)
        level_across = jnp.where(across_at % levels == l, value, level_across)
    vert = jnp.exp(-jnp.abs(level_down - level_across) / vertical_scale)
    vert = jnp.where(down_at // levels == across_at // levels, vert, 0.0)

    lane = lax.broadcasted_iota(jnp.int32, (1, width), 1)

    def live(block):
        return (lane < count_ref[block]).astype(jnp.float32)

    def lift_copy(which, src, dst, n):
        return pltpu.make_async_remote_copy(
            src_ref=table.at[:, cols(src, src + n)],
            dst_ref=table.at[:, cols(dst, dst + n)],
            send_sem=lift_send.at[which],
            recv_sem=lift_recv.at[which],
            device_id={"grid": down},
            device_id_type=MESH,
        )

    lift_copies = [
        lift_copy(0, 0, own, extra),
        lift_copy(1, extra, own + extra, own - extra),
        lift_copy(2, own, 2 * own, extra),
    ]

    def far_copy(which, src, dst_ref, n):
        return pltpu.make_async_remote_copy(
            src_ref=far.at[:, cols(src, src + n)],
            dst_ref=dst_ref,
            send_sem=far_send.at[which],
            recv_sem=far_recv.at[which],
            device_id={"grid": up},
            device_id_type=MESH,
        )

    far_copies = [
        far_copy(0, own, relay_in, extra),
        far_copy(1, extra, near_in.at[:, cols(extra, own)], own - extra),
        far_copy(2, 0, near_in.at[:, cols(0, extra)], extra),
    ]

    greeted = False
    for part in range(parts):
        loads[part][0].wait()
        loads[part][1].wait()
        at = cols(part * step, (part + 1) * step)
        mask = jnp.concatenate([live(part * step + s) for s in range(step)], axis=1)
        masked = [control[t, :, at] * mask for t in range(slots)]
        for g in range(members // group):
            weighted = []
            for m in range(g * group, (g + 1) * group):
                total = ens[m, 0, :, at].astype(jnp.float32) * masked[0]
                for t in range(1, slots):
                    total = total + ens[m, t, :, at].astype(jnp.float32) * masked[t]
                weighted.append(total)
            lifted = jnp.dot(
                vert,
                jnp.concatenate(weighted, axis=0),
                precision=lax.Precision.HIGHEST,
                preferred_element_type=jnp.float32,
            )
            table[g * size : (g + 1) * size, at] = lifted.astype(table.dtype)
        if not greeted:
            pl.semaphore_wait(barrier, 2 + peers - 1)
            greeted = True
        if part * step < extra <= (part + 1) * step:
            lift_copies[0].start()
    lift_copies[1].start()
    load_loc.wait()

    def pair(i, k):
        return loc[slot_ref[i * (SPAN + 1) + k]]

    def from_below(j, first, last):
        stack = jnp.concatenate([pair(i, j - i) for i in range(first, last)], axis=0)
        return jnp.dot(table[:, cols(first, last)], stack, preferred_element_type=jnp.float32)

    def from_above(j, first, last):
        stack = jnp.concatenate([pair(j, s - j) for s in range(first, last)], axis=1)
        return lax.dot_general(
            table[:, cols(first, last)],
            stack,
            (((1,), (1,)), ((), ())),
            preferred_element_type=jnp.float32,
        )

    for j in range(2 * own, own + SPAN):
        far[:, cols(j - own, j - own + 1)] = from_below(j, j - SPAN, own).astype(far.dtype)
    far_copies[0].start()
    for j in range(own + extra, 2 * own):
        far[:, cols(j - own, j - own + 1)] = from_below(j, j - SPAN, own).astype(far.dtype)
    far_copies[1].start()

    lift_copies[0].wait_recv()
    lift_copies[2].start()

    far_copies[0].wait_recv()
    for j in range(own, own + extra):
        first = max(0, j - SPAN)
        total = from_below(j, first, own) + relay_in[:, cols(j - own, j - own + 1)].astype(
            jnp.float32
        )
        far[:, cols(j - own, j - own + 1)] = total.astype(far.dtype)
    far_copies[2].start()

    for j in range(own):
        total = from_above(j, j, own)
        if j > 0:
            total = total + from_below(j, 0, j)
        spread[:, cols(j, j + 1)] = total

    lift_copies[1].wait_recv()
    for j in range(own):
        last = min(2 * own, j + SPAN + 1)
        spread[:, cols(j, j + 1)] += from_above(j, own, last)

    chunk = own // peers

    def finish(j):
        column = cols(j, j + 1)
        total = spread[:, column] + near_in[:, column].astype(jnp.float32)
        if j + SPAN >= 2 * own:
            total = total + from_above(j, 2 * own, j + SPAN + 1)
        scale = live(j) / (members * peers - 1)
        within = cols(j % chunk, j % chunk + 1)
        for t in range(slots):
            mixed = ens[0, t, :, column].astype(jnp.float32) * total[:levels]
            for m in range(1, members):
                mixed = mixed + ens[m, t, :, column].astype(jnp.float32) * (
                    total[m * levels : (m + 1) * levels]
                )
            terms[j // chunk, t, :, within] = mixed * scale

    def term_copy(to):
        return pltpu.make_async_remote_copy(
            src_ref=terms.at[to],
            dst_ref=terms_in.at[mem],
            send_sem=term_send.at[to],
            recv_sem=term_recv.at[mem],
            device_id={"mem": jnp.int32(to)},
            device_id_type=MESH,
        )

    far_copies[1].wait_recv()
    lift_copies[2].wait_recv()
    arrived = False
    for to in reversed(range(peers)):
        if to * chunk < extra and not arrived:
            far_copies[2].wait_recv()
            arrived = True
        for j in range(to * chunk, (to + 1) * chunk):
            finish(j)

        @pl.when(mem != to)
        def _():
            term_copy(to).start()

        @pl.when(mem == to)
        def _():
            terms_in[to] = terms[to]

    for source in range(peers):

        @pl.when(mem != source)
        def _():
            pltpu.make_async_remote_copy(
                src_ref=terms.at[source],
                dst_ref=terms_in.at[source],
                send_sem=term_send.at[source],
                recv_sem=term_recv.at[source],
                device_id={"mem": jnp.int32(source)},
                device_id_type=MESH,
            ).wait()

    result = terms_in[0]
    for source in range(1, peers):
        result = result + terms_in[source]
    out_ref[...] = result
    for copy in lift_copies + far_copies:
        copy.wait_send()


def per_device(ens, control, col_count, level_index, pair_blocks, loc_blocks):
    own = col_count.shape[0]
    width = loc_blocks.shape[1]
    pairs = pair_blocks.shape[0]
    per_block = pairs // own
    devices = lax.axis_size("grid")
    peers = lax.axis_size("mem")
    members, slots, levels, columns = ens.shape
    rows = members * levels
    assert own < SPAN <= 2 * own and own % peers == 0 and devices > 2
    extra = SPAN - own

    offsets = jnp.mod(pair_blocks[:, 1] - pair_blocks[:, 0], own * devices)
    offsets = offsets.reshape(own, 1, per_block)
    wanted = jnp.arange(SPAN + 1, dtype=jnp.int32).reshape(1, SPAN + 1, 1)
    place = jnp.arange(pairs, dtype=jnp.int32).reshape(own, 1, per_block)
    slot = jnp.min(jnp.where(offsets == wanted, place, pairs), axis=2).reshape(-1)

    smem = pl.BlockSpec(memory_space=pltpu.SMEM)
    anywhere = pl.BlockSpec(memory_space=pl.ANY)
    parts = own // 2 if own % 2 == 0 else own
    sizes = (members, slots, levels, own, width, devices, peers)
    share = columns // peers
    return pl.pallas_call(
        functools.partial(kernel, sizes),
        out_shape=jax.ShapeDtypeStruct((slots, levels, share), jnp.float32),
        in_specs=[smem, smem, smem, anywhere, anywhere, anywhere],
        out_specs=pl.BlockSpec(memory_space=pltpu.VMEM),
        scratch_shapes=[
            pltpu.VMEM(ens.shape, ens.dtype),
            pltpu.VMEM(control.shape, control.dtype),
            pltpu.VMEM((pairs + 1, width, width), loc_blocks.dtype),
            pltpu.VMEM((rows, (own + SPAN) * width), jnp.bfloat16),
            pltpu.VMEM((rows, SPAN * width), jnp.bfloat16),
            pltpu.VMEM((rows, extra * width), jnp.bfloat16),
            pltpu.VMEM((rows, columns), jnp.bfloat16),
            pltpu.VMEM((rows, columns), jnp.float32),
            pltpu.VMEM((peers, slots, levels, share), jnp.float32),
            pltpu.VMEM((peers, slots, levels, share), jnp.float32),
            pltpu.SemaphoreType.DMA((2 * parts + 1,)),
            pltpu.SemaphoreType.DMA((3,)),
            pltpu.SemaphoreType.DMA((3,)),
            pltpu.SemaphoreType.DMA((3,)),
            pltpu.SemaphoreType.DMA((3,)),
            pltpu.SemaphoreType.DMA((peers,)),
            pltpu.SemaphoreType.DMA((peers,)),
        ],
        compiler_params=pltpu.CompilerParams(
            collective_id=0, has_side_effects=True, vmem_limit_bytes=48 * 1024 * 1024
        ),
        cost_estimate=pl.CostEstimate(
            flops=2 * rows * width * width * pairs * 2,
            bytes_accessed=ens.size * 2 + control.size * 4 + loc_blocks.size * 2,
            transcendentals=0,
        ),
    )(col_count, level_index, slot, ens, control, loc_blocks)


def solution(mesh):
    return jax.shard_map(
        per_device,
        mesh=mesh,
        in_specs=(
            P("mem", None, None, "grid"),
            P(None, None, "grid"),
            P("grid"),
            P(),
            P("grid", None),
            P("grid", None, None),
        ),
        out_specs=P(None, None, ("grid", "mem")),
        check_vma=False,
    )
```

```python
import functools

import jax
import jax.numpy as jnp
from jax import lax
from jax.experimental import pallas as pl
from jax.experimental.pallas import tpu as pltpu
from jax.sharding import PartitionSpec as P

SPAN = 12
MESH = pl.DeviceIdType.MESH


vertical_scale = 8.0


def kernel(
    sizes,
    count_hbm,
    level_hbm,
    pair_hbm,
    ens_hbm,
    control_hbm,
    loc_hbm,
    out_ref,
    counts,
    level_at,
    listed,
    slot,
    ens,
    control,
    loc,
    table,
    far,
    relay_in,
    near_in,
    spread,
    terms,
    terms_in,
    small_sems,
    in_sems,
    lift_send,
    lift_recv,
    far_send,
    far_recv,
    term_send,
    term_recv,
):
    members, slots, levels, own, width, devices, peers = sizes
    extra = SPAN - own
    pairs = loc_hbm.shape[0]
    per_block = pairs // own
    here = lax.axis_index("grid")
    mem = lax.axis_index("mem")
    up = lax.rem(here + 1, devices)
    down = lax.rem(here + devices - 1, devices)
    parts = own // 2

    def cols(first, last):
        return slice(first * width, last * width)

    small = [
        pltpu.make_async_copy(level_hbm, level_at, small_sems.at[0]),
        pltpu.make_async_copy(count_hbm, counts, small_sems.at[1]),
        pltpu.make_async_copy(pair_hbm, listed, small_sems.at[2]),
    ]
    for copy in small:
        copy.start()
    loads = []
    for part in range(parts):
        at = cols(2 * part, 2 * part + 2)
        a = pltpu.make_async_copy(
            control_hbm.at[:, :, at], control.at[:, :, at], in_sems.at[2 * part]
        )
        b = pltpu.make_async_copy(
            ens_hbm.at[:, :, :, at], ens.at[:, :, :, at], in_sems.at[2 * part + 1]
        )
        a.start()
        b.start()
        loads.append((a, b))
    load_loc = pltpu.make_async_copy(loc_hbm, loc.at[pl.ds(0, pairs)], in_sems.at[2 * parts])
    load_loc.start()

    barrier = pltpu.get_barrier_semaphore()
    for other in (up, down):
        pl.semaphore_signal(barrier, inc=1, device_id={"grid": other}, device_id_type=MESH)
    for away in range(1, peers):
        pl.semaphore_signal(
            barrier, inc=1, device_id={"mem": lax.rem(mem + away, peers)}, device_id_type=MESH
        )

    loc[pairs] = jnp.zeros((width, width), loc.dtype)

    group = max(g for g in range(1, members + 1) if members % g == 0 and g * levels <= 256)
    size = group * levels
    down_at = lax.broadcasted_iota(jnp.int32, (size, 1), 0)
    across_at = lax.broadcasted_iota(jnp.int32, (1, size), 1)
    level_down = jnp.zeros((size, 1), jnp.float32)
    level_across = jnp.zeros((1, size), jnp.float32)
    for copy in small:
        copy.wait()
    for l in range(levels):
        value = level_at[l].astype(jnp.float32)
        level_down = jnp.where(down_at % levels == l, value, level_down)
        level_across = jnp.where(across_at % levels == l, value, level_across)
    vert = jnp.exp(-jnp.abs(level_down - level_across) / vertical_scale)
    vert = jnp.where(down_at // levels == across_at // levels, vert, 0.0)

    low = 7
    for b in range(own):
        first_word = jnp.int32(0)
        second_word = jnp.int32(0)
        for p in range(per_block):
            k = listed[1, b * per_block + p] - listed[0, b * per_block + p]
            k = jnp.where(k < 0, k + own * devices, k)
            near = k < low
            code = jnp.int32(p + 1) << (4 * jnp.where(near, k, k - low))
            first_word = first_word + jnp.where(near, code, 0)
            second_word = second_word + jnp.where(near, 0, code)
        for k in range(SPAN + 1):
            word = first_word >> (4 * k) if k < low else second_word >> (4 * (k - low))
            place = word & 15
            at = jnp.minimum(b * per_block + place - 1, pairs)
            slot[b * (SPAN + 1) + k] = jnp.where(place == 0, pairs, at)

    lane = lax.broadcasted_iota(jnp.int32, (1, width), 1)

    def live(block):
        return (lane < counts[block]).astype(jnp.float32)

    def lift_copy(which, src, dst, n):
        return pltpu.make_async_remote_copy(
            src_ref=table.at[:, cols(src, src + n)],
            dst_ref=table.at[:, cols(dst, dst + n)],
            send_sem=lift_send.at[which],
            recv_sem=lift_recv.at[which],
            device_id={"grid": down},
            device_id_type=MESH,
        )

    lift_own = [lift_copy(part, 2 * part, own + 2 * part, 2) for part in range(parts)]
    lift_relay = [lift_copy(parts + n, own + n, 2 * own + n, 1) for n in range(extra)]

    def far_copy(which, src, dst_ref, n):
        return pltpu.make_async_remote_copy(
            src_ref=far.at[:, cols(src, src + n)],
            dst_ref=dst_ref,
            send_sem=far_send.at[which],
            recv_sem=far_recv.at[which],
            device_id={"grid": up},
            device_id_type=MESH,
        )

    far_two = {
        n: far_copy(n // 2, own + n, relay_in.at[:, cols(n, n + 2)], 2)
        for n in range(0, extra, 2)
    }
    far_mid = {
        n: far_copy(n // 2, n, near_in.at[:, cols(n, n + 2)], 2) for n in range(extra, own, 2)
    }
    far_last = [
        far_copy(parts + n, n, near_in.at[:, cols(n, n + 1)], 1) for n in range(extra)
    ]

    def pair(i, k, least):
        return loc[slot[i * (SPAN + 1) + k] if least <= k <= SPAN else pairs]

    def from_below(j, n, first, last):
        stack = jnp.concatenate(
            [
                jnp.concatenate([pair(i, j + c - i, 1) for i in range(first, last)], axis=0)
                for c in range(n)
            ],
            axis=1,
        )
        return jnp.dot(table[:, cols(first, last)], stack, preferred_element_type=jnp.float32)

    def from_above(j, n, first, last):
        stack = jnp.concatenate(
            [
                jnp.concatenate([pair(j + c, s - j - c, 0) for s in range(first, last)], axis=1)
                for c in range(n)
            ],
            axis=0,
        )
        return lax.dot_general(
            table[:, cols(first, last)],
            stack,
            (((1,), (1,)), ((), ())),
            preferred_element_type=jnp.float32,
        )

    def lift(part):
        loads[part][0].wait()
        loads[part][1].wait()
        at = cols(2 * part, 2 * part + 2)
        mask = jnp.concatenate([live(2 * part), live(2 * part + 1)], axis=1)
        masked = [control[t, :, at] * mask for t in range(slots)]
        for g in range(members // group):
            weighted = []
            for m in range(g * group, (g + 1) * group):
                total = ens[m, 0, :, at].astype(jnp.float32) * masked[0]
                for t in range(1, slots):
                    total = total + ens[m, t, :, at].astype(jnp.float32) * masked[t]
                weighted.append(total)
            lifted = jnp.dot(
                vert,
                jnp.concatenate(weighted, axis=0),
                precision=lax.Precision.HIGHEST,
                preferred_element_type=jnp.float32,
            )
            table[g * size : (g + 1) * size, at] = lifted.astype(table.dtype)

    for part in range(parts):
        lift(part)
        if part == 0:
            pl.semaphore_wait(barrier, 2 + peers - 1)
        lift_own[part].start()
    load_loc.wait()

    for n in range(0, extra, 2):
        j = 2 * own + n
        far[:, cols(j - own, j - own + 2)] = from_below(j, 2, j - SPAN, own).astype(far.dtype)
        far_two[n].start()
    for n in range(extra, own, 2):
        j = own + n
        far[:, cols(n, n + 2)] = from_below(j, 2, j - SPAN, own).astype(far.dtype)
        far_mid[n].start()

    for part in range(extra // 2):
        lift_own[part].wait_recv()
        for n in (2 * part, 2 * part + 1):
            lift_relay[n].start()

    for n in range(0, extra, 2):
        far_two[n].wait_recv()
        j = own + n
        total = from_below(j, 2, max(0, j - SPAN), own)
        total = total + relay_in[:, cols(n, n + 2)].astype(jnp.float32)
        far[:, cols(n, n + 2)] = total.astype(far.dtype)
        far_last[n].start()
        far_last[n + 1].start()

    for j in range(0, own, 2):
        spread[:, cols(j, j + 2)] = from_above(j, 2, j, own) + from_below(j, 2, 0, j + 1)

    for part in range(parts):
        if part >= extra // 2:
            lift_own[part].wait_recv()
        source = own + 2 * part
        for j in range(0, own, 2):
            if source <= j + 1 + SPAN:
                spread[:, cols(j, j + 2)] += from_above(j, 2, source, source + 2)

    chunk = own // peers

    def finish(j):
        column = cols(j, j + 1)
        total = spread[:, column] + near_in[:, column].astype(jnp.float32)
        if j + SPAN >= 2 * own:
            total = total + from_above(j, 1, 2 * own, j + SPAN + 1)
        scale = live(j) / (members * peers - 1)
        for t in range(slots):
            mixed = ens[0, t, :, column].astype(jnp.float32) * total[:levels]
            for m in range(1, members):
                mixed = mixed + ens[m, t, :, column].astype(jnp.float32) * (
                    total[m * levels : (m + 1) * levels]
                )
            terms[j, t] = mixed * scale
        to = j // chunk

        @pl.when(mem != to)
        def _():
            pltpu.make_async_remote_copy(
                src_ref=terms.at[j],
                dst_ref=terms_in.at[mem, j % chunk],
                send_sem=term_send.at[j],
                recv_sem=term_recv.at[mem, j % chunk],
                device_id={"mem": jnp.int32(to)},
                device_id_type=MESH,
            ).start()

        @pl.when(mem == to)
        def _():
            terms_in[to, j % chunk] = terms[j]

    waiting = dict(far_mid)
    for n in range(max(extra, own - extra)):
        j = extra + n
        if j < own:
            if j in waiting:
                waiting.pop(j).wait_recv()
            if j + SPAN >= 2 * own:
                lift_relay[j + SPAN - 2 * own].wait_recv()
            finish(j)
        if n < extra:
            far_last[n].wait_recv()
            finish(n)

    for q in range(chunk):
        for source in range(peers):

            @pl.when(mem != source)
            def _():
                pltpu.make_async_remote_copy(
                    src_ref=terms.at[source * chunk + q],
                    dst_ref=terms_in.at[source, q],
                    send_sem=term_send.at[source * chunk + q],
                    recv_sem=term_recv.at[source, q],
                    device_id={"mem": jnp.int32(source)},
                    device_id_type=MESH,
                ).wait()

        result = terms_in[0, q]
        for source in range(1, peers):
            result = result + terms_in[source, q]
        out_ref[:, :, cols(q, q + 1)] = result
    for copy in (
        lift_own + lift_relay + list(far_two.values()) + list(far_mid.values()) + far_last
    ):
        copy.wait_send()


def per_device(ens, control, col_count, level_index, pair_blocks, loc_blocks):
    own = col_count.shape[0]
    width = loc_blocks.shape[1]
    pairs = pair_blocks.shape[0]
    devices = lax.axis_size("grid")
    peers = lax.axis_size("mem")
    members, slots, levels, columns = ens.shape
    rows = members * levels
    extra = SPAN - own
    assert 0 < extra <= own and own % peers == 0 and devices > 2
    assert own % 2 == 0 and extra % 2 == 0 and pairs // own < 16

    parts = own // 2
    chunk = own // peers
    sizes = (members, slots, levels, own, width, devices, peers)
    dma = pltpu.SemaphoreType.DMA
    return pl.pallas_call(
        functools.partial(kernel, sizes),
        out_shape=jax.ShapeDtypeStruct((slots, levels, columns // peers), jnp.float32),
        in_specs=[pl.BlockSpec(memory_space=pltpu.HBM)] * 6,
        out_specs=pl.BlockSpec(memory_space=pltpu.VMEM),
        scratch_shapes=[
            pltpu.SMEM(col_count.shape, jnp.int32),
            pltpu.SMEM(level_index.shape, jnp.int32),
            pltpu.SMEM((2, pairs), jnp.int32),
            pltpu.SMEM((own * (SPAN + 1),), jnp.int32),
            pltpu.VMEM(ens.shape, ens.dtype),
            pltpu.VMEM(control.shape, control.dtype),
            pltpu.VMEM((pairs + 1, width, width), loc_blocks.dtype),
            pltpu.VMEM((rows, (own + SPAN) * width), jnp.bfloat16),
            pltpu.VMEM((rows, SPAN * width), jnp.bfloat16),
            pltpu.VMEM((rows, extra * width), jnp.bfloat16),
            pltpu.VMEM((rows, columns), jnp.bfloat16),
            pltpu.VMEM((rows, columns), jnp.float32),
            pltpu.VMEM((own, slots, levels, width), jnp.float32),
            pltpu.VMEM((peers, chunk, slots, levels, width), jnp.float32),
            dma((3,)),
            dma((2 * parts + 1,)),
            dma((parts + extra,)),
            dma((parts + extra,)),
            dma((parts + extra,)),
            dma((parts + extra,)),
            dma((own,)),
            dma((peers, chunk)),
        ],
        compiler_params=pltpu.CompilerParams(
            collective_id=0, has_side_effects=True, vmem_limit_bytes=56 * 1024 * 1024
        ),
        cost_estimate=pl.CostEstimate(
            flops=2 * rows * width * width * pairs * 2,
            bytes_accessed=ens.size * 2 + control.size * 4 + loc_blocks.size * 2,
            transcendentals=0,
        ),
    )(col_count, level_index, pair_blocks.T, ens, control, loc_blocks)


def solution(mesh):
    return jax.shard_map(
        per_device,
        mesh=mesh,
        in_specs=(
            P("mem", None, None, "grid"),
            P(None, None, "grid"),
            P("grid"),
            P(),
            P("grid", None),
            P("grid", None, None),
        ),
        out_specs=P(None, None, ("grid", "mem")),
        check_vma=False,
    )
```

```python
import functools

import jax
import jax.numpy as jnp
from jax import lax
from jax.experimental import pallas as pl
from jax.experimental.pallas import tpu as pltpu
from jax.sharding import PartitionSpec as P

SPAN = 12
MESH = pl.DeviceIdType.MESH


vertical_scale = 8.0


def pieces_of(own):
    return [(0, 1), (1, 1)] + [(first, 2) for first in range(2, own, 2)]


def kernel(
    sizes,
    count_hbm,
    level_hbm,
    pair_hbm,
    ens_hbm,
    control_hbm,
    loc_hbm,
    out_ref,
    counts,
    level_at,
    listed,
    slot,
    ens,
    control,
    loc,
    table,
    far,
    relay_in,
    near_in,
    spread,
    terms,
    terms_in,
    small_sems,
    loc_sem,
    in_sems,
    lift_send,
    lift_recv,
    far_send,
    far_recv,
    term_send,
    term_recv,
):
    members, slots, levels, own, width, devices, peers = sizes
    extra = SPAN - own
    pairs = loc_hbm.shape[0]
    per_block = pairs // own
    here = lax.axis_index("grid")
    mem = lax.axis_index("mem")
    up = lax.rem(here + 1, devices)
    down = lax.rem(here + devices - 1, devices)
    pieces = pieces_of(own)

    def cols(first, last):
        return slice(first * width, last * width)

    small = [
        pltpu.make_async_copy(level_hbm, level_at, small_sems.at[0]),
        pltpu.make_async_copy(count_hbm, counts, small_sems.at[1]),
    ]
    load_pairs = pltpu.make_async_copy(pair_hbm, listed, small_sems.at[2])
    load_loc = pltpu.make_async_copy(loc_hbm, loc.at[pl.ds(0, pairs)], loc_sem)
    loads = {}
    for first, n in pieces:
        at = cols(first, first + n)
        loads[first] = (
            pltpu.make_async_copy(
                control_hbm.at[:, :, at], control.at[:, :, at], in_sems.at[2 * first]
            ),
            pltpu.make_async_copy(
                ens_hbm.at[:, :, :, at], ens.at[:, :, :, at], in_sems.at[2 * first + 1]
            ),
        )
    for copy in small:
        copy.start()
    for first, n in pieces[:2]:
        for copy in loads[first]:
            copy.start()

    barrier = pltpu.get_barrier_semaphore()
    for other in (up, down):
        pl.semaphore_signal(barrier, inc=1, device_id={"grid": other}, device_id_type=MESH)
    for away in range(1, peers):
        pl.semaphore_signal(
            barrier, inc=1, device_id={"mem": lax.rem(mem + away, peers)}, device_id_type=MESH
        )

    loc[pairs] = jnp.zeros((width, width), loc.dtype)

    group = max(g for g in range(1, members + 1) if members % g == 0 and g * levels <= 256)
    size = group * levels
    down_at = lax.broadcasted_iota(jnp.int32, (size, 1), 0)
    across_at = lax.broadcasted_iota(jnp.int32, (1, size), 1)
    level_down = jnp.zeros((size, 1), jnp.float32)
    level_across = jnp.zeros((1, size), jnp.float32)
    for copy in small:
        copy.wait()
    for l in range(levels):
        value = level_at[l].astype(jnp.float32)
        level_down = jnp.where(down_at % levels == l, value, level_down)
        level_across = jnp.where(across_at % levels == l, value, level_across)
    vert = jnp.exp(-jnp.abs(level_down - level_across) / vertical_scale)
    vert = jnp.where(down_at // levels == across_at // levels, vert, 0.0)

    lane = lax.broadcasted_iota(jnp.int32, (1, width), 1)

    def live(block):
        return (lane < counts[block]).astype(jnp.float32)

    def lift_copy(which, src, dst, n):
        return pltpu.make_async_remote_copy(
            src_ref=table.at[pl.ds(src, n)],
            dst_ref=table.at[pl.ds(dst, n)],
            send_sem=lift_send.at[which],
            recv_sem=lift_recv.at[which],
            device_id={"grid": down},
            device_id_type=MESH,
        )

    lift_own = {first: lift_copy(first, first, own + first, n) for first, n in pieces}
    lift_relay = [lift_copy(own + n, own + n, 2 * own + n, 1) for n in range(extra)]
    due = dict(lift_own)

    def arrive(last):
        for first in [f for f in due if f < last]:
            due.pop(first).wait_recv()

    def far_copy(which, src, dst_ref, n):
        return pltpu.make_async_remote_copy(
            src_ref=far.at[pl.ds(src, n)],
            dst_ref=dst_ref,
            send_sem=far_send.at[which],
            recv_sem=far_recv.at[which],
            device_id={"grid": up},
            device_id_type=MESH,
        )

    far_two = {
        n: far_copy(own + n, own + n, relay_in.at[pl.ds(n, 2)], 2) for n in range(0, extra, 2)
    }
    far_mid = {n: far_copy(n, n, near_in.at[pl.ds(n, 2)], 2) for n in range(extra, own, 2)}
    far_last = [far_copy(n, n, near_in.at[pl.ds(n, 1)], 1) for n in range(extra)]

    def pair(i, k, least):
        return loc[slot[i * (SPAN + 1) + k] if least <= k <= SPAN else pairs]

    def blocks(first, last):
        return jnp.concatenate([table[b] for b in range(first, last)], axis=1)

    def from_below(j, n, first, last):
        stack = jnp.concatenate(
            [
                jnp.concatenate([pair(i, j + c - i, 1) for i in range(first, last)], axis=0)
                for c in range(n)
            ],
            axis=1,
        )
        return jnp.dot(blocks(first, last), stack, preferred_element_type=jnp.float32)

    def from_above(j, n, first, last):
        stack = jnp.concatenate(
            [
                jnp.concatenate([pair(j + c, s - j - c, 0) for s in range(first, last)], axis=1)
                for c in range(n)
            ],
            axis=0,
        )
        return lax.dot_general(
            blocks(first, last),
            stack,
            (((1,), (1,)), ((), ())),
            preferred_element_type=jnp.float32,
        )

    def lift(first, n):
        for copy in loads[first]:
            copy.wait()
        at = cols(first, first + n)
        mask = jnp.concatenate([live(first + c) for c in range(n)], axis=1)
        masked = [control[t, :, at] * mask for t in range(slots)]
        for g in range(members // group):
            weighted = []
            for m in range(g * group, (g + 1) * group):
                total = ens[m, 0, :, at].astype(jnp.float32) * masked[0]
                for t in range(1, slots):
                    total = total + ens[m, t, :, at].astype(jnp.float32) * masked[t]
                weighted.append(total)
            lifted = jnp.dot(
                vert,
                jnp.concatenate(weighted, axis=0),
                precision=lax.Precision.HIGHEST,
                preferred_element_type=jnp.float32,
            )
            for c in range(n):
                table[first + c, g * size : (g + 1) * size] = lifted[:, cols(c, c + 1)].astype(
                    table.dtype
                )

    for first, n in pieces:
        lift(first, n)
        if first == 0:
            for later, n in pieces[2:]:
                for copy in loads[later]:
                    copy.start()
            load_pairs.start()
            load_loc.start()
            pl.semaphore_wait(barrier, 2 + peers - 1)
        lift_own[first].start()

    load_pairs.wait()
    low = 7
    for b in range(own):
        first_word = jnp.int32(0)
        second_word = jnp.int32(0)
        for p in range(per_block):
            k = listed[1, b * per_block + p] - listed[0, b * per_block + p]
            k = jnp.where(k < 0, k + own * devices, k)
            near = k < low
            code = jnp.int32(p + 1) << (4 * jnp.where(near, k, k - low))
            first_word = first_word + jnp.where(near, code, 0)
            second_word = second_word + jnp.where(near, 0, code)
        for k in range(SPAN + 1):
            word = first_word >> (4 * k) if k < low else second_word >> (4 * (k - low))
            place = word & 15
            at = jnp.minimum(b * per_block + place - 1, pairs)
            slot[b * (SPAN + 1) + k] = jnp.where(place == 0, pairs, at)

    load_loc.wait()

    def keep_far(at, total):
        for c in range(2):
            far[at + c] = total[:, cols(c, c + 1)].astype(far.dtype)

    for n in range(0, extra, 2):
        j = 2 * own + n
        keep_far(own + n, from_below(j, 2, j - SPAN, own))
        far_two[n].start()
    for n in range(extra, own, 2):
        j = own + n
        keep_far(n, from_below(j, 2, j - SPAN, own))
        far_mid[n].start()

    for n in range(extra):
        arrive(n + 1)
        lift_relay[n].start()

    for n in range(0, extra, 2):
        j = own + n
        total = from_below(j, 2, max(0, j - SPAN), own)
        far_two[n].wait_recv()
        passing = jnp.concatenate([relay_in[n], relay_in[n + 1]], axis=1)
        keep_far(n, total + passing.astype(jnp.float32))
        far_last[n].start()
        far_last[n + 1].start()

    for j in range(0, own, 2):
        spread[:, cols(j, j + 2)] = from_above(j, 2, j, own) + from_below(j, 2, 0, j + 1)

    for first in range(0, own, 2):
        arrive(first + 2)
        source = own + first
        for j in range(0, own, 2):
            if source <= j + 1 + SPAN:
                spread[:, cols(j, j + 2)] += from_above(j, 2, source, source + 2)

    chunk = own // peers

    def finish(j):
        column = cols(j, j + 1)
        total = spread[:, column] + near_in[j].astype(jnp.float32)
        if j + SPAN >= 2 * own:
            total = total + from_above(j, 1, 2 * own, j + SPAN + 1)
        scale = live(j) / (members * peers - 1)
        for t in range(slots):
            mixed = ens[0, t, :, column].astype(jnp.float32) * total[:levels]
            for m in range(1, members):
                mixed = mixed + ens[m, t, :, column].astype(jnp.float32) * (
                    total[m * levels : (m + 1) * levels]
                )
            terms[j, t] = mixed * scale
        to = j // chunk

        @pl.when(mem != to)
        def _():
            pltpu.make_async_remote_copy(
                src_ref=terms.at[j],
                dst_ref=terms_in.at[mem, j % chunk],
                send_sem=term_send.at[j],
                recv_sem=term_recv.at[mem, j % chunk],
                device_id={"mem": jnp.int32(to)},
                device_id_type=MESH,
            ).start()

        @pl.when(mem == to)
        def _():
            terms_in[to, j % chunk] = terms[j]

    waiting = dict(far_mid)
    for n in range(max(extra, own - extra)):
        j = extra + n
        if j < own:
            if j in waiting:
                waiting.pop(j).wait_recv()
            if j + SPAN >= 2 * own:
                lift_relay[j + SPAN - 2 * own].wait_recv()
            finish(j)
        if n < extra:
            far_last[n].wait_recv()
            finish(n)

    for q in range(chunk):
        for source in range(peers):

            @pl.when(mem != source)
            def _():
                pltpu.make_async_remote_copy(
                    src_ref=terms.at[source * chunk + q],
                    dst_ref=terms_in.at[source, q],
                    send_sem=term_send.at[source * chunk + q],
                    recv_sem=term_recv.at[source, q],
                    device_id={"mem": jnp.int32(source)},
                    device_id_type=MESH,
                ).wait()

        result = terms_in[0, q]
        for source in range(1, peers):
            result = result + terms_in[source, q]
        out_ref[:, :, cols(q, q + 1)] = result
    for copy in (
        list(lift_own.values()) + lift_relay + list(far_two.values()) + list(far_mid.values()) + far_last
    ):
        copy.wait_send()


def per_device(ens, control, col_count, level_index, pair_blocks, loc_blocks):
    own = col_count.shape[0]
    width = loc_blocks.shape[1]
    pairs = pair_blocks.shape[0]
    devices = lax.axis_size("grid")
    peers = lax.axis_size("mem")
    members, slots, levels, columns = ens.shape
    rows = members * levels
    extra = SPAN - own
    assert 0 < extra <= own and own % peers == 0 and devices > 2
    assert own % 2 == 0 and extra % 2 == 0 and pairs // own < 16

    chunk = own // peers
    sizes = (members, slots, levels, own, width, devices, peers)
    dma = pltpu.SemaphoreType.DMA
    return pl.pallas_call(
        functools.partial(kernel, sizes),
        out_shape=jax.ShapeDtypeStruct((slots, levels, columns // peers), jnp.float32),
        in_specs=[pl.BlockSpec(memory_space=pltpu.HBM)] * 6,
        out_specs=pl.BlockSpec(memory_space=pltpu.VMEM),
        scratch_shapes=[
            pltpu.SMEM(col_count.shape, jnp.int32),
            pltpu.SMEM(level_index.shape, jnp.int32),
            pltpu.SMEM((2, pairs), jnp.int32),
            pltpu.SMEM((own * (SPAN + 1),), jnp.int32),
            pltpu.VMEM(ens.shape, ens.dtype),
            pltpu.VMEM(control.shape, control.dtype),
            pltpu.VMEM((pairs + 1, width, width), loc_blocks.dtype),
            pltpu.VMEM((own + SPAN, rows, width), jnp.bfloat16),
            pltpu.VMEM((SPAN, rows, width), jnp.bfloat16),
            pltpu.VMEM((extra, rows, width), jnp.bfloat16),
            pltpu.VMEM((own, rows, width), jnp.bfloat16),
            pltpu.VMEM((rows, columns), jnp.float32),
            pltpu.VMEM((own, slots, levels, width), jnp.float32),
            pltpu.VMEM((peers, chunk, slots, levels, width), jnp.float32),
            dma((3,)),
            dma,
            dma((2 * own,)),
            dma((SPAN,)),
            dma((SPAN,)),
            dma((SPAN,)),
            dma((SPAN,)),
            dma((own,)),
            dma((peers, chunk)),
        ],
        compiler_params=pltpu.CompilerParams(
            collective_id=0, has_side_effects=True, vmem_limit_bytes=56 * 1024 * 1024
        ),
        cost_estimate=pl.CostEstimate(
            flops=2 * rows * width * width * pairs * 2,
            bytes_accessed=ens.size * 2 + control.size * 4 + loc_blocks.size * 2,
            transcendentals=0,
        ),
    )(col_count, level_index, pair_blocks.T, ens, control, loc_blocks)


def solution(mesh):
    return jax.shard_map(
        per_device,
        mesh=mesh,
        in_specs=(
            P("mem", None, None, "grid"),
            P(None, None, "grid"),
            P("grid"),
            P(),
            P("grid", None),
            P("grid", None, None),
        ),
        out_specs=P(None, None, ("grid", "mem")),
        check_vma=False,
    )
```

```python
import functools

import jax
import jax.numpy as jnp
from jax import lax
from jax.experimental import pallas as pl
from jax.experimental.pallas import tpu as pltpu
from jax.sharding import PartitionSpec as P

SPAN = 12
MESH = pl.DeviceIdType.MESH


vertical_scale = 8.0


def pieces_of(own):
    return [(0, 1), (1, 1)] + [(first, 2) for first in range(2, own, 2)]


def kernel(
    sizes,
    count_hbm,
    level_hbm,
    pair_hbm,
    ens_hbm,
    control_hbm,
    loc_hbm,
    out_ref,
    counts,
    level_at,
    listed,
    slot,
    ens,
    control,
    loc,
    table,
    far,
    relay_in,
    near_in,
    spread,
    terms,
    terms_in,
    small_sems,
    loc_sem,
    in_sems,
    lift_send,
    lift_recv,
    far_send,
    far_recv,
    term_send,
    term_recv,
):
    members, slots, levels, own, width, devices, peers = sizes
    extra = SPAN - own
    pairs = loc_hbm.shape[0]
    per_block = pairs // own
    here = lax.axis_index("grid")
    mem = lax.axis_index("mem")
    up = lax.rem(here + 1, devices)
    down = lax.rem(here + devices - 1, devices)
    pieces = pieces_of(own)

    def cols(first, last):
        return slice(first * width, last * width)

    small = [
        pltpu.make_async_copy(level_hbm, level_at, small_sems.at[0]),
        pltpu.make_async_copy(count_hbm, counts, small_sems.at[1]),
    ]
    load_pairs = pltpu.make_async_copy(pair_hbm, listed, small_sems.at[2])
    load_loc = pltpu.make_async_copy(loc_hbm, loc.at[pl.ds(0, pairs)], loc_sem)
    loads = {}
    for first, n in pieces:
        at = cols(first, first + n)
        loads[first] = (
            pltpu.make_async_copy(
                control_hbm.at[:, :, at], control.at[:, :, at], in_sems.at[2 * first]
            ),
            pltpu.make_async_copy(
                ens_hbm.at[:, :, :, at], ens.at[:, :, :, at], in_sems.at[2 * first + 1]
            ),
        )
    for copy in small:
        copy.start()
    for first, n in pieces[:2]:
        for copy in loads[first]:
            copy.start()

    barrier = pltpu.get_barrier_semaphore()
    for other in (up, down):
        pl.semaphore_signal(barrier, inc=1, device_id={"grid": other}, device_id_type=MESH)
    for away in range(1, peers):
        pl.semaphore_signal(
            barrier, inc=1, device_id={"mem": lax.rem(mem + away, peers)}, device_id_type=MESH
        )

    loc[pairs] = jnp.zeros((width, width), loc.dtype)

    group = max(g for g in range(1, members + 1) if members % g == 0 and g * levels <= 256)
    size = group * levels
    down_at = lax.broadcasted_iota(jnp.int32, (size, 1), 0)
    across_at = lax.broadcasted_iota(jnp.int32, (1, size), 1)
    level_down = jnp.zeros((size, 1), jnp.float32)
    level_across = jnp.zeros((1, size), jnp.float32)
    for copy in small:
        copy.wait()
    for l in range(levels):
        value = level_at[l].astype(jnp.float32)
        level_down = jnp.where(down_at % levels == l, value, level_down)
        level_across = jnp.where(across_at % levels == l, value, level_across)
    vert = jnp.exp(-jnp.abs(level_down - level_across) / vertical_scale)
    vert = jnp.where(down_at // levels == across_at // levels, vert, 0.0)

    lane = lax.broadcasted_iota(jnp.int32, (1, width), 1)

    def live(block):
        return (lane < counts[block]).astype(jnp.float32)

    def lift_copy(which, src, dst, n):
        return pltpu.make_async_remote_copy(
            src_ref=table.at[pl.ds(src, n)],
            dst_ref=table.at[pl.ds(dst, n)],
            send_sem=lift_send.at[which],
            recv_sem=lift_recv.at[which],
            device_id={"grid": down},
            device_id_type=MESH,
        )

    lift_own = {first: lift_copy(first, first, own + first, n) for first, n in pieces}
    lift_relay = [lift_copy(own + n, own + n, 2 * own + n, 1) for n in range(extra)]
    due = dict(lift_own)

    def arrive(last):
        for first in [f for f in due if f < last]:
            due.pop(first).wait_recv()

    def far_copy(which, src, dst_ref, n):
        return pltpu.make_async_remote_copy(
            src_ref=far.at[pl.ds(src, n)],
            dst_ref=dst_ref,
            send_sem=far_send.at[which],
            recv_sem=far_recv.at[which],
            device_id={"grid": up},
            device_id_type=MESH,
        )

    far_two = {
        n: far_copy(own + n, own + n, relay_in.at[pl.ds(n, 2)], 2) for n in range(0, extra, 2)
    }
    far_mid = {n: far_copy(n, n, near_in.at[pl.ds(n, 2)], 2) for n in range(extra, own, 2)}
    far_last = [far_copy(n, n, near_in.at[pl.ds(n, 1)], 1) for n in range(extra)]

    def pair(i, k, least):
        return loc[slot[i * (SPAN + 1) + k] if least <= k <= SPAN else pairs]

    def blocks(first, last):
        return jnp.concatenate([table[b] for b in range(first, last)], axis=1)

    def from_below(j, n, first, last):
        stack = jnp.concatenate(
            [
                jnp.concatenate([pair(i, j + c - i, 1) for i in range(first, last)], axis=0)
                for c in range(n)
            ],
            axis=1,
        )
        return jnp.dot(blocks(first, last), stack, preferred_element_type=jnp.float32)

    def from_above(j, n, first, last):
        stack = jnp.concatenate(
            [
                jnp.concatenate([pair(j + c, s - j - c, 0) for s in range(first, last)], axis=1)
                for c in range(n)
            ],
            axis=0,
        )
        return lax.dot_general(
            blocks(first, last),
            stack,
            (((1,), (1,)), ((), ())),
            preferred_element_type=jnp.float32,
        )

    def lift(first, n):
        for copy in loads[first]:
            copy.wait()
        at = cols(first, first + n)
        mask = jnp.concatenate([live(first + c) for c in range(n)], axis=1)
        masked = [control[t, :, at] * mask for t in range(slots)]
        for g in range(members // group):
            weighted = []
            for m in range(g * group, (g + 1) * group):
                total = ens[m, 0, :, at].astype(jnp.float32) * masked[0]
                for t in range(1, slots):
                    total = total + ens[m, t, :, at].astype(jnp.float32) * masked[t]
                weighted.append(total)
            lifted = jnp.dot(
                vert,
                jnp.concatenate(weighted, axis=0),
                precision=lax.Precision.HIGHEST,
                preferred_element_type=jnp.float32,
            )
            for c in range(n):
                table[first + c, g * size : (g + 1) * size] = lifted[:, cols(c, c + 1)].astype(
                    table.dtype
                )

    for first, n in pieces:
        lift(first, n)
        if first == 0:
            for later, n in pieces[2:]:
                for copy in loads[later]:
                    copy.start()
            load_pairs.start()
            load_loc.start()
            pl.semaphore_wait(barrier, 2 + peers - 1)
        lift_own[first].start()

    load_pairs.wait()
    low = 7
    for b in range(own):
        first_word = jnp.int32(0)
        second_word = jnp.int32(0)
        for p in range(per_block):
            k = listed[1, b * per_block + p] - listed[0, b * per_block + p]
            k = jnp.where(k < 0, k + own * devices, k)
            near = k < low
            code = jnp.int32(p + 1) << (4 * jnp.where(near, k, k - low))
            first_word = first_word + jnp.where(near, code, 0)
            second_word = second_word + jnp.where(near, 0, code)
        for k in range(SPAN + 1):
            word = first_word >> (4 * k) if k < low else second_word >> (4 * (k - low))
            place = word & 15
            at = jnp.minimum(b * per_block + place - 1, pairs)
            slot[b * (SPAN + 1) + k] = jnp.where(place == 0, pairs, at)

    load_loc.wait()

    def keep_far(at, total):
        for c in range(2):
            far[at + c] = total[:, cols(c, c + 1)].astype(far.dtype)

    for n in range(0, extra, 2):
        j = 2 * own + n
        keep_far(own + n, from_below(j, 2, j - SPAN, own))
        far_two[n].start()
    for n in range(extra, own, 2):
        j = own + n
        keep_far(n, from_below(j, 2, j - SPAN, own))
        far_mid[n].start()

    for n in range(extra):
        arrive(n + 1)
        lift_relay[n].start()

    for n in range(0, extra, 2):
        j = own + n
        total = from_below(j, 2, max(0, j - SPAN), own)
        far_two[n].wait_recv()
        passing = jnp.concatenate([relay_in[n], relay_in[n + 1]], axis=1)
        keep_far(n, total + passing.astype(jnp.float32))
        far_last[n].start()
        far_last[n + 1].start()

    for j in range(0, own, 2):
        spread[:, cols(j, j + 2)] = from_above(j, 2, j, own) + from_below(j, 2, 0, j + 1)

    for first in range(0, own, 2):
        arrive(first + 2)
        source = own + first
        for j in range(0, own, 2):
            if source <= j + 1 + SPAN:
                spread[:, cols(j, j + 2)] += from_above(j, 2, source, source + 2)

    chunk = own // peers

    def finish(j):
        column = cols(j, j + 1)
        total = spread[:, column] + near_in[j].astype(jnp.float32)
        if j + SPAN >= 2 * own:
            total = total + from_above(j, 1, 2 * own, j + SPAN + 1)
        scale = live(j) / (members * peers - 1)
        for t in range(slots):
            mixed = ens[0, t, :, column].astype(jnp.float32) * total[:levels]
            for m in range(1, members):
                mixed = mixed + ens[m, t, :, column].astype(jnp.float32) * (
                    total[m * levels : (m + 1) * levels]
                )
            terms[j, t] = mixed * scale
        to = j // chunk

        @pl.when(mem != to)
        def _():
            pltpu.make_async_remote_copy(
                src_ref=terms.at[j],
                dst_ref=terms_in.at[mem, j % chunk],
                send_sem=term_send.at[j],
                recv_sem=term_recv.at[mem, j % chunk],
                device_id={"mem": jnp.int32(to)},
                device_id_type=MESH,
            ).start()

        @pl.when(mem == to)
        def _():
            terms_in[to, j % chunk] = terms[j]

    waiting = dict(far_mid)
    for n in range(max(extra, own - extra)):
        j = extra + n
        if j < own:
            if j in waiting:
                waiting.pop(j).wait_recv()
            if j + SPAN >= 2 * own:
                lift_relay[j + SPAN - 2 * own].wait_recv()
            finish(j)
        if n < extra:
            far_last[n].wait_recv()
            finish(n)

    for q in range(chunk):
        for source in range(peers):

            @pl.when(mem != source)
            def _():
                pltpu.make_async_remote_copy(
                    src_ref=terms.at[source * chunk + q],
                    dst_ref=terms_in.at[source, q],
                    send_sem=term_send.at[source * chunk + q],
                    recv_sem=term_recv.at[source, q],
                    device_id={"mem": jnp.int32(source)},
                    device_id_type=MESH,
                ).wait()

        result = terms_in[0, q]
        for source in range(1, peers):
            result = result + terms_in[source, q]
        out_ref[:, :, cols(q, q + 1)] = result
    for copy in (
        list(lift_own.values()) + lift_relay + list(far_two.values()) + list(far_mid.values()) + far_last
    ):
        copy.wait_send()


def per_device(ens, control, col_count, level_index, pair_blocks, loc_blocks):
    own = col_count.shape[0]
    width = loc_blocks.shape[1]
    pairs = pair_blocks.shape[0]
    devices = lax.axis_size("grid")
    peers = lax.axis_size("mem")
    members, slots, levels, columns = ens.shape
    rows = members * levels
    extra = SPAN - own
    assert 0 < extra <= own and own % peers == 0 and devices > 2
    assert own % 2 == 0 and extra % 2 == 0 and pairs // own < 16

    chunk = own // peers
    sizes = (members, slots, levels, own, width, devices, peers)
    dma = pltpu.SemaphoreType.DMA
    operands = (col_count, level_index, pair_blocks.T, ens, control, loc_blocks)
    return pl.pallas_call(
        functools.partial(kernel, sizes),
        out_shape=jax.ShapeDtypeStruct((slots, levels, columns // peers), jnp.float32),
        in_specs=[pl.BlockSpec(memory_space=pltpu.HBM)] * 6,
        out_specs=pl.BlockSpec(memory_space=pltpu.VMEM),
        scratch_shapes=[
            pltpu.SMEM(col_count.shape, jnp.int32),
            pltpu.SMEM(level_index.shape, jnp.int32),
            pltpu.SMEM((2, pairs), jnp.int32),
            pltpu.SMEM((own * (SPAN + 1),), jnp.int32),
            pltpu.VMEM(ens.shape, ens.dtype),
            pltpu.VMEM(control.shape, control.dtype),
            pltpu.VMEM((pairs + 1, width, width), loc_blocks.dtype),
            pltpu.VMEM((own + SPAN, rows, width), jnp.bfloat16),
            pltpu.VMEM((SPAN, rows, width), jnp.bfloat16),
            pltpu.VMEM((extra, rows, width), jnp.bfloat16),
            pltpu.VMEM((own, rows, width), jnp.bfloat16),
            pltpu.VMEM((rows, columns), jnp.float32),
            pltpu.VMEM((own, slots, levels, width), jnp.float32),
            pltpu.VMEM((peers, chunk, slots, levels, width), jnp.float32),
            dma((3,)),
            dma,
            dma((2 * own,)),
            dma((SPAN,)),
            dma((SPAN,)),
            dma((SPAN,)),
            dma((SPAN,)),
            dma((own,)),
            dma((peers, chunk)),
        ],
        compiler_params=pltpu.CompilerParams(
            collective_id=0, has_side_effects=True, vmem_limit_bytes=32 * 1024 * 1024
        ),
        cost_estimate=pl.CostEstimate(
            flops=2 * rows * width * width * pairs * 2,
            bytes_accessed=ens.size * 2 + control.size * 4 + loc_blocks.size * 2,
            transcendentals=0,
        ),
    )(*[pltpu.with_memory_space_constraint(array, pltpu.HBM) for array in operands])


def solution(mesh):
    return jax.shard_map(
        per_device,
        mesh=mesh,
        in_specs=(
            P("mem", None, None, "grid"),
            P(None, None, "grid"),
            P("grid"),
            P(),
            P("grid", None),
            P("grid", None, None),
        ),
        out_specs=P(None, None, ("grid", "mem")),
        check_vma=False,
    )
```

```python
import functools

import jax
import jax.numpy as jnp
from jax import lax
from jax.experimental import pallas as pl
from jax.experimental.pallas import tpu as pltpu
from jax.sharding import PartitionSpec as P

SPAN = 12
MESH = pl.DeviceIdType.MESH


vertical_scale = 8.0


def pieces_of(own):
    return [(first, 2) for first in range(0, own, 2)]


def messages_of(count):
    return [(first, 2) for first in range(0, count - 2, 2)] + [(count - 2, 1), (count - 1, 1)]


def kernel(
    sizes,
    count_hbm,
    level_hbm,
    pair_hbm,
    ens_hbm,
    control_hbm,
    loc_hbm,
    out_ref,
    counts,
    level_at,
    listed,
    slot,
    ens,
    control,
    loc,
    table,
    far,
    relay_in,
    near_in,
    spread,
    terms,
    terms_in,
    small_sems,
    loc_sem,
    in_sems,
    lift_send,
    lift_recv,
    far_send,
    far_recv,
    term_send,
    term_recv,
):
    members, slots, levels, own, width, devices, peers = sizes
    extra = SPAN - own
    pairs = loc_hbm.shape[0]
    per_block = pairs // own
    here = lax.axis_index("grid")
    mem = lax.axis_index("mem")
    up = lax.rem(here + 1, devices)
    down = lax.rem(here + devices - 1, devices)
    pieces = pieces_of(own)

    def cols(first, last):
        return slice(first * width, last * width)

    small = [
        pltpu.make_async_copy(level_hbm, level_at, small_sems.at[0]),
        pltpu.make_async_copy(count_hbm, counts, small_sems.at[1]),
    ]
    load_pairs = pltpu.make_async_copy(pair_hbm, listed, small_sems.at[2])
    load_loc = pltpu.make_async_copy(loc_hbm, loc.at[pl.ds(0, pairs)], loc_sem)
    loads = {}
    for first, n in pieces:
        at = cols(first, first + n)
        loads[first] = (
            pltpu.make_async_copy(
                control_hbm.at[:, :, at], control.at[:, :, at], in_sems.at[2 * first]
            ),
            pltpu.make_async_copy(
                ens_hbm.at[:, :, :, at], ens.at[:, :, :, at], in_sems.at[2 * first + 1]
            ),
        )
    for copy in small:
        copy.start()
    for first, n in pieces[:2]:
        for copy in loads[first]:
            copy.start()

    barrier = pltpu.get_barrier_semaphore()
    for other in (up, down):
        pl.semaphore_signal(barrier, inc=1, device_id={"grid": other}, device_id_type=MESH)
    for away in range(1, peers):
        pl.semaphore_signal(
            barrier, inc=1, device_id={"mem": lax.rem(mem + away, peers)}, device_id_type=MESH
        )

    loc[pairs] = jnp.zeros((width, width), loc.dtype)

    group = max(g for g in range(1, members + 1) if members % g == 0 and g * levels <= 256)
    size = group * levels
    down_at = lax.broadcasted_iota(jnp.int32, (size, 1), 0)
    across_at = lax.broadcasted_iota(jnp.int32, (1, size), 1)
    level_down = jnp.zeros((size, 1), jnp.float32)
    level_across = jnp.zeros((1, size), jnp.float32)
    for copy in small:
        copy.wait()
    for l in range(levels):
        value = level_at[l].astype(jnp.float32)
        level_down = jnp.where(down_at % levels == l, value, level_down)
        level_across = jnp.where(across_at % levels == l, value, level_across)
    vert = jnp.exp(-jnp.abs(level_down - level_across) / vertical_scale)
    vert = jnp.where(down_at // levels == across_at // levels, vert, 0.0)

    lane = lax.broadcasted_iota(jnp.int32, (1, width), 1)

    def live(block):
        return (lane < counts[block]).astype(jnp.float32)

    def lift_copy(which, src, dst, n):
        return pltpu.make_async_remote_copy(
            src_ref=table.at[pl.ds(src, n)],
            dst_ref=table.at[pl.ds(dst, n)],
            send_sem=lift_send.at[which],
            recv_sem=lift_recv.at[which],
            device_id={"grid": down},
            device_id_type=MESH,
        )

    near_part = [(first, 2) for first in range(0, extra, 2)]
    far_part = [(extra, own - extra)] if own > extra else []
    lift_own = {
        first: lift_copy(first, first, own + first, n) for first, n in near_part + far_part
    }
    lift_relay = {
        first: lift_copy(own + first, own + first, 2 * own + first, n)
        for first, n in messages_of(extra)
    }
    due = dict(lift_own)
    due_relay = dict(lift_relay)

    def arrive(last, waiting=due):
        for first in [f for f in waiting if f < last]:
            waiting.pop(first).wait_recv()

    def far_copy(which, src, dst_ref, n):
        return pltpu.make_async_remote_copy(
            src_ref=far.at[pl.ds(src, n)],
            dst_ref=dst_ref,
            send_sem=far_send.at[which],
            recv_sem=far_recv.at[which],
            device_id={"grid": up},
            device_id_type=MESH,
        )

    far_two = far_copy(own, own, relay_in, extra)
    far_mid = {
        first: far_copy(first, first, near_in.at[pl.ds(first, n)], n) for first, n in far_part
    }
    far_last = {
        first: far_copy(first, first, near_in.at[pl.ds(first, n)], n)
        for first, n in messages_of(extra)
    }
    due_far = dict(far_last)
    due_mid = dict(far_mid)

    def pair(i, k, least):
        return loc[slot[i * (SPAN + 1) + k] if least <= k <= SPAN else pairs]

    def blocks(first, last):
        return jnp.concatenate([table[b] for b in range(first, last)], axis=1)

    def from_below(j, n, first, last):
        stack = jnp.concatenate(
            [
                jnp.concatenate([pair(i, j + c - i, 1) for i in range(first, last)], axis=0)
                for c in range(n)
            ],
            axis=1,
        )
        return jnp.dot(blocks(first, last), stack, preferred_element_type=jnp.float32)

    def from_above(j, n, first, last):
        stack = jnp.concatenate(
            [
                jnp.concatenate([pair(j + c, s - j - c, 0) for s in range(first, last)], axis=1)
                for c in range(n)
            ],
            axis=0,
        )
        return lax.dot_general(
            blocks(first, last),
            stack,
            (((1,), (1,)), ((), ())),
            preferred_element_type=jnp.float32,
        )

    def lift(first, n):
        for copy in loads[first]:
            copy.wait()
        at = cols(first, first + n)
        mask = jnp.concatenate([live(first + c) for c in range(n)], axis=1)
        masked = [control[t, :, at] * mask for t in range(slots)]
        for g in range(members // group):
            weighted = []
            for m in range(g * group, (g + 1) * group):
                total = ens[m, 0, :, at].astype(jnp.float32) * masked[0]
                for t in range(1, slots):
                    total = total + ens[m, t, :, at].astype(jnp.float32) * masked[t]
                weighted.append(total)
            lifted = jnp.dot(
                vert,
                jnp.concatenate(weighted, axis=0),
                precision=lax.Precision.HIGHEST,
                preferred_element_type=jnp.float32,
            )
            for c in range(n):
                table[first + c, g * size : (g + 1) * size] = lifted[:, cols(c, c + 1)].astype(
                    table.dtype
                )

    for first, n in pieces:
        lift(first, n)
        if first == 0:
            for later, unused in pieces[2:]:
                for copy in loads[later]:
                    copy.start()
            load_pairs.start()
            load_loc.start()
            pl.semaphore_wait(barrier, 2 + peers - 1)
        if first in lift_own and first < extra:
            lift_own[first].start()
    for first, n in far_part:
        lift_own[first].start()

    load_pairs.wait()
    low = 7
    for b in range(own):
        first_word = jnp.int32(0)
        second_word = jnp.int32(0)
        for p in range(per_block):
            k = listed[1, b * per_block + p] - listed[0, b * per_block + p]
            k = jnp.where(k < 0, k + own * devices, k)
            near = k < low
            code = jnp.int32(p + 1) << (4 * jnp.where(near, k, k - low))
            first_word = first_word + jnp.where(near, code, 0)
            second_word = second_word + jnp.where(near, 0, code)
        for k in range(SPAN + 1):
            word = first_word >> (4 * k) if k < low else second_word >> (4 * (k - low))
            place = word & 15
            at = jnp.minimum(b * per_block + place - 1, pairs)
            slot[b * (SPAN + 1) + k] = jnp.where(place == 0, pairs, at)

    load_loc.wait()

    def keep_far(at, total):
        for c in range(2):
            far[at + c] = total[:, cols(c, c + 1)].astype(far.dtype)

    for n in range(0, extra, 2):
        j = 2 * own + n
        keep_far(own + n, from_below(j, 2, j - SPAN, own))
    far_two.start()
    for n in range(extra, own, 2):
        j = own + n
        keep_far(n, from_below(j, 2, j - SPAN, own))
    for copy in far_mid.values():
        copy.start()

    for first, n in messages_of(extra):
        arrive(first + n)
        lift_relay[first].start()

    for n in range(0, extra, 2):
        j = own + n
        total = from_below(j, 2, max(0, j - SPAN), own)
        if n == 0:
            far_two.wait_recv()
        passing = jnp.concatenate([relay_in[n], relay_in[n + 1]], axis=1)
        keep_far(n, total + passing.astype(jnp.float32))
        for at in (n, n + 1):
            if at in far_last:
                far_last[at].start()

    for j in range(0, own, 2):
        spread[:, cols(j, j + 2)] = from_above(j, 2, j, own) + from_below(j, 2, 0, j + 1)

    for first in range(0, own, 2):
        arrive(first + 2)
        source = own + first
        for j in range(0, own, 2):
            if source <= j + 1 + SPAN:
                spread[:, cols(j, j + 2)] += from_above(j, 2, source, source + 2)

    chunk = own // peers

    def finish(j):
        column = cols(j, j + 1)
        total = spread[:, column] + near_in[j].astype(jnp.float32)
        if j + SPAN >= 2 * own:
            total = total + from_above(j, 1, 2 * own, j + SPAN + 1)
        scale = live(j) / (members * peers - 1)
        for t in range(slots):
            mixed = ens[0, t, :, column].astype(jnp.float32) * total[:levels]
            for m in range(1, members):
                mixed = mixed + ens[m, t, :, column].astype(jnp.float32) * (
                    total[m * levels : (m + 1) * levels]
                )
            terms[j, t] = mixed * scale
        to = j // chunk

        @pl.when(mem != to)
        def _():
            pltpu.make_async_remote_copy(
                src_ref=terms.at[j],
                dst_ref=terms_in.at[mem, j % chunk],
                send_sem=term_send.at[j],
                recv_sem=term_recv.at[mem, j % chunk],
                device_id={"mem": jnp.int32(to)},
                device_id_type=MESH,
            ).start()

        @pl.when(mem == to)
        def _():
            terms_in[to, j % chunk] = terms[j]

    order = []
    for n in range(max(extra, own - extra)):
        order += [b for b in (extra + n, n) if extra <= b < own or b == n < extra]

    def finish_after(j, relays, lasts):
        if j >= extra:
            arrive(j + 1, due_mid)
            arrive(j + SPAN - 2 * own + 1, relays)
        else:
            arrive(j + 1, lasts)
        finish(j)

    for j in order[:-2]:
        finish_after(j, due_relay, due_far)
    first_core = lax.rem(here, 2) == 0
    for turn, chosen in ((order[-2:], first_core), (order[:-3:-1], jnp.logical_not(first_core))):

        @pl.when(chosen)
        def _():
            relays, lasts = dict(due_relay), dict(due_far)
            for j in turn:
                finish_after(j, relays, lasts)

    for q in range(chunk):
        for source in range(peers):

            @pl.when(mem != source)
            def _():
                pltpu.make_async_remote_copy(
                    src_ref=terms.at[source * chunk + q],
                    dst_ref=terms_in.at[source, q],
                    send_sem=term_send.at[source * chunk + q],
                    recv_sem=term_recv.at[source, q],
                    device_id={"mem": jnp.int32(source)},
                    device_id_type=MESH,
                ).wait()

        result = terms_in[0, q]
        for source in range(1, peers):
            result = result + terms_in[source, q]
        out_ref[:, :, cols(q, q + 1)] = result
    for group_of in (lift_own, lift_relay, far_mid, far_last):
        for copy in group_of.values():
            copy.wait_send()
    far_two.wait_send()


def per_device(ens, control, col_count, level_index, pair_blocks, loc_blocks):
    own = col_count.shape[0]
    width = loc_blocks.shape[1]
    pairs = pair_blocks.shape[0]
    devices = lax.axis_size("grid")
    peers = lax.axis_size("mem")
    members, slots, levels, columns = ens.shape
    rows = members * levels
    extra = SPAN - own
    assert 0 < extra <= own and own % peers == 0 and devices > 2
    assert own % 2 == 0 and extra % 2 == 0 and pairs // own < 16

    chunk = own // peers
    sizes = (members, slots, levels, own, width, devices, peers)
    dma = pltpu.SemaphoreType.DMA
    operands = (col_count, level_index, pair_blocks.T, ens, control, loc_blocks)
    return pl.pallas_call(
        functools.partial(kernel, sizes),
        out_shape=jax.ShapeDtypeStruct((slots, levels, columns // peers), jnp.float32),
        in_specs=[pl.BlockSpec(memory_space=pltpu.HBM)] * 6,
        out_specs=pl.BlockSpec(memory_space=pltpu.VMEM),
        scratch_shapes=[
            pltpu.SMEM(col_count.shape, jnp.int32),
            pltpu.SMEM(level_index.shape, jnp.int32),
            pltpu.SMEM((2, pairs), jnp.int32),
            pltpu.SMEM((own * (SPAN + 1),), jnp.int32),
            pltpu.VMEM(ens.shape, ens.dtype),
            pltpu.VMEM(control.shape, control.dtype),
            pltpu.VMEM((pairs + 1, width, width), loc_blocks.dtype),
            pltpu.VMEM((own + SPAN, rows, width), jnp.bfloat16),
            pltpu.VMEM((SPAN, rows, width), jnp.bfloat16),
            pltpu.VMEM((extra, rows, width), jnp.bfloat16),
            pltpu.VMEM((own, rows, width), jnp.bfloat16),
            pltpu.VMEM((rows, columns), jnp.float32),
            pltpu.VMEM((own, slots, levels, width), jnp.float32),
            pltpu.VMEM((peers, chunk, slots, levels, width), jnp.float32),
            dma((3,)),
            dma,
            dma((2 * own,)),
            dma((SPAN,)),
            dma((SPAN,)),
            dma((SPAN,)),
            dma((SPAN,)),
            dma((own,)),
            dma((peers, chunk)),
        ],
        compiler_params=pltpu.CompilerParams(
            collective_id=0, has_side_effects=True, vmem_limit_bytes=32 * 1024 * 1024
        ),
        cost_estimate=pl.CostEstimate(
            flops=2 * rows * width * width * pairs * 2,
            bytes_accessed=ens.size * 2 + control.size * 4 + loc_blocks.size * 2,
            transcendentals=0,
        ),
    )(*[pltpu.with_memory_space_constraint(array, pltpu.HBM) for array in operands])


def solution(mesh):
    return jax.shard_map(
        per_device,
        mesh=mesh,
        in_specs=(
            P("mem", None, None, "grid"),
            P(None, None, "grid"),
            P("grid"),
            P(),
            P("grid", None),
            P("grid", None, None),
        ),
        out_specs=P(None, None, ("grid", "mem")),
        check_vma=False,
    )
```

```python
import functools

import jax
import jax.numpy as jnp
from jax import lax
from jax.experimental import pallas as pl
from jax.experimental.pallas import tpu as pltpu
from jax.sharding import PartitionSpec as P

SPAN = 12
MESH = pl.DeviceIdType.MESH


vertical_scale = 8.0


def pieces_of(own):
    return [(first, 2) for first in range(0, own, 2)]


def messages_of(count):
    return [(first, 1) for first in range(count)]


def kernel(
    sizes,
    count_hbm,
    level_hbm,
    pair_hbm,
    ens_hbm,
    control_hbm,
    loc_hbm,
    out_ref,
    counts,
    level_at,
    listed,
    slot,
    ens,
    control,
    loc,
    table,
    far,
    relay_in,
    near_in,
    spread,
    terms,
    terms_in,
    small_sems,
    loc_sem,
    in_sems,
    lift_send,
    lift_recv,
    far_send,
    far_recv,
    term_send,
    term_recv,
):
    members, slots, levels, own, width, devices, peers = sizes
    extra = SPAN - own
    pairs = loc_hbm.shape[0]
    per_block = pairs // own
    here = lax.axis_index("grid")
    mem = lax.axis_index("mem")
    up = lax.rem(here + 1, devices)
    down = lax.rem(here + devices - 1, devices)
    pieces = pieces_of(own)

    def cols(first, last):
        return slice(first * width, last * width)

    small = [
        pltpu.make_async_copy(level_hbm, level_at, small_sems.at[0]),
        pltpu.make_async_copy(count_hbm, counts, small_sems.at[1]),
    ]
    load_pairs = pltpu.make_async_copy(pair_hbm, listed, small_sems.at[2])
    load_loc = pltpu.make_async_copy(loc_hbm, loc.at[pl.ds(0, pairs)], loc_sem)
    loads = {}
    for first, n in pieces:
        at = cols(first, first + n)
        loads[first] = (
            pltpu.make_async_copy(
                control_hbm.at[:, :, at], control.at[:, :, at], in_sems.at[2 * first]
            ),
            pltpu.make_async_copy(
                ens_hbm.at[:, :, :, at], ens.at[:, :, :, at], in_sems.at[2 * first + 1]
            ),
        )
    for copy in small:
        copy.start()
    for first, n in pieces[:2]:
        for copy in loads[first]:
            copy.start()

    barrier = pltpu.get_barrier_semaphore()
    for other in (up, down):
        pl.semaphore_signal(barrier, inc=1, device_id={"grid": other}, device_id_type=MESH)
    for away in range(1, peers):
        pl.semaphore_signal(
            barrier, inc=1, device_id={"mem": lax.rem(mem + away, peers)}, device_id_type=MESH
        )

    loc[pairs] = jnp.zeros((width, width), loc.dtype)

    group = max(g for g in range(1, members + 1) if members % g == 0 and g * levels <= 256)
    size = group * levels
    down_at = lax.broadcasted_iota(jnp.int32, (size, 1), 0)
    across_at = lax.broadcasted_iota(jnp.int32, (1, size), 1)
    level_down = jnp.zeros((size, 1), jnp.float32)
    level_across = jnp.zeros((1, size), jnp.float32)
    for copy in small:
        copy.wait()
    for l in range(levels):
        value = level_at[l].astype(jnp.float32)
        level_down = jnp.where(down_at % levels == l, value, level_down)
        level_across = jnp.where(across_at % levels == l, value, level_across)
    vert = jnp.exp(-jnp.abs(level_down - level_across) / vertical_scale)
    vert = jnp.where(down_at // levels == across_at // levels, vert, 0.0)

    lane = lax.broadcasted_iota(jnp.int32, (1, width), 1)

    def live(block):
        return (lane < counts[block]).astype(jnp.float32)

    def lift_copy(which, src, dst, n):
        return pltpu.make_async_remote_copy(
            src_ref=table.at[pl.ds(src, n)],
            dst_ref=table.at[pl.ds(dst, n)],
            send_sem=lift_send.at[which],
            recv_sem=lift_recv.at[which],
            device_id={"grid": down},
            device_id_type=MESH,
        )

    near_part = [(first, 2) for first in range(0, extra, 2)]
    far_part = [(first, 2) for first in range(extra, own, 2)]
    lift_own = {
        first: lift_copy(first, first, own + first, n) for first, n in near_part + far_part
    }
    lift_relay = {
        first: lift_copy(own + first, own + first, 2 * own + first, n)
        for first, n in messages_of(extra)
    }
    due = dict(lift_own)
    due_relay = dict(lift_relay)

    def arrive(last, waiting=due):
        for first in [f for f in waiting if f < last]:
            waiting.pop(first).wait_recv()

    def far_copy(which, src, dst_ref, n):
        return pltpu.make_async_remote_copy(
            src_ref=far.at[pl.ds(src, n)],
            dst_ref=dst_ref,
            send_sem=far_send.at[which],
            recv_sem=far_recv.at[which],
            device_id={"grid": up},
            device_id_type=MESH,
        )

    far_two = far_copy(own, own, relay_in, extra)
    far_mid = {
        first: far_copy(first, first, near_in.at[pl.ds(first, n)], n) for first, n in far_part
    }
    far_last = {
        first: far_copy(first, first, near_in.at[pl.ds(first, n)], n)
        for first, n in messages_of(extra)
    }
    due_far = dict(far_last)
    due_mid = dict(far_mid)

    def pair(i, k, least):
        return loc[slot[i * (SPAN + 1) + k] if least <= k <= SPAN else pairs]

    def blocks(first, last):
        return jnp.concatenate([table[b] for b in range(first, last)], axis=1)

    def from_below(j, n, first, last):
        stack = jnp.concatenate(
            [
                jnp.concatenate([pair(i, j + c - i, 1) for i in range(first, last)], axis=0)
                for c in range(n)
            ],
            axis=1,
        )
        return jnp.dot(blocks(first, last), stack, preferred_element_type=jnp.float32)

    def from_above(j, n, first, last):
        stack = jnp.concatenate(
            [
                jnp.concatenate([pair(j + c, s - j - c, 0) for s in range(first, last)], axis=1)
                for c in range(n)
            ],
            axis=0,
        )
        return lax.dot_general(
            blocks(first, last),
            stack,
            (((1,), (1,)), ((), ())),
            preferred_element_type=jnp.float32,
        )

    def lift(first, n):
        for copy in loads[first]:
            copy.wait()
        at = cols(first, first + n)
        mask = jnp.concatenate([live(first + c) for c in range(n)], axis=1)
        masked = [control[t, :, at] * mask for t in range(slots)]
        for g in range(members // group):
            weighted = []
            for m in range(g * group, (g + 1) * group):
                total = ens[m, 0, :, at].astype(jnp.float32) * masked[0]
                for t in range(1, slots):
                    total = total + ens[m, t, :, at].astype(jnp.float32) * masked[t]
                weighted.append(total)
            lifted = jnp.dot(
                vert,
                jnp.concatenate(weighted, axis=0),
                precision=lax.Precision.HIGHEST,
                preferred_element_type=jnp.float32,
            )
            for c in range(n):
                table[first + c, g * size : (g + 1) * size] = lifted[:, cols(c, c + 1)].astype(
                    table.dtype
                )

    for first, n in pieces:
        lift(first, n)
        if first == 0:
            for later, unused in pieces[2:]:
                for copy in loads[later]:
                    copy.start()
            load_pairs.start()
            load_loc.start()
            pl.semaphore_wait(barrier, 2 + peers - 1)
        lift_own[first].start()

    load_pairs.wait()
    low = 7
    for b in range(own):
        first_word = jnp.int32(0)
        second_word = jnp.int32(0)
        for p in range(per_block):
            k = listed[1, b * per_block + p] - listed[0, b * per_block + p]
            k = jnp.where(k < 0, k + own * devices, k)
            near = k < low
            code = jnp.int32(p + 1) << (4 * jnp.where(near, k, k - low))
            first_word = first_word + jnp.where(near, code, 0)
            second_word = second_word + jnp.where(near, 0, code)
        for k in range(SPAN + 1):
            word = first_word >> (4 * k) if k < low else second_word >> (4 * (k - low))
            place = word & 15
            at = jnp.minimum(b * per_block + place - 1, pairs)
            slot[b * (SPAN + 1) + k] = jnp.where(place == 0, pairs, at)

    load_loc.wait()

    def keep_far(at, total):
        for c in range(2):
            far[at + c] = total[:, cols(c, c + 1)].astype(far.dtype)

    for n in range(0, extra, 2):
        j = 2 * own + n
        keep_far(own + n, from_below(j, 2, j - SPAN, own))
    far_two.start()
    for n in range(extra, own, 2):
        j = own + n
        keep_far(n, from_below(j, 2, j - SPAN, own))
        far_mid[n].start()

    for first, n in messages_of(extra):
        arrive(first + n)
        lift_relay[first].start()

    for n in range(0, extra, 2):
        j = own + n
        total = from_below(j, 2, max(0, j - SPAN), own)
        if n == 0:
            far_two.wait_recv()
        passing = jnp.concatenate([relay_in[n], relay_in[n + 1]], axis=1)
        keep_far(n, total + passing.astype(jnp.float32))
        for at in (n, n + 1):
            if at in far_last:
                far_last[at].start()

    for j in range(0, own, 2):
        spread[:, cols(j, j + 2)] = from_above(j, 2, j, own) + from_below(j, 2, 0, j + 1)

    for first in range(0, own, 2):
        arrive(first + 2)
        source = own + first
        for j in range(0, own, 2):
            if source <= j + 1 + SPAN:
                spread[:, cols(j, j + 2)] += from_above(j, 2, source, source + 2)

    chunk = own // peers

    def finish(j):
        column = cols(j, j + 1)
        total = spread[:, column] + near_in[j].astype(jnp.float32)
        scale = live(j) / (members * peers - 1)
        for t in range(slots):
            mixed = ens[0, t, :, column].astype(jnp.float32) * total[:levels]
            for m in range(1, members):
                mixed = mixed + ens[m, t, :, column].astype(jnp.float32) * (
                    total[m * levels : (m + 1) * levels]
                )
            terms[j, t] = mixed * scale
        to = j // chunk

        @pl.when(mem != to)
        def _():
            pltpu.make_async_remote_copy(
                src_ref=terms.at[j],
                dst_ref=terms_in.at[mem, j % chunk],
                send_sem=term_send.at[j],
                recv_sem=term_recv.at[mem, j % chunk],
                device_id={"mem": jnp.int32(to)},
                device_id_type=MESH,
            ).start()

        @pl.when(mem == to)
        def _():
            terms_in[to, j % chunk] = terms[j]

    order = []
    for n in range(max(extra, own - extra)):
        order += [b for b in (extra + n, n) if extra <= b < own or b == n < extra]

    def finish_after(j, relays, lasts):
        if j >= extra:
            arrive(j + 1, due_mid)
            reached = j + SPAN - 2 * own
            arrive(reached + 1, relays)
            spread[:, cols(j, j + 1)] += from_above(
                j, 1, 2 * own + reached - reached % 2, 2 * own + reached + 1
            )
            if reached % 2 == 1:
                for later in range(j + 1, own):
                    spread[:, cols(later, later + 1)] += from_above(
                        later, 1, 2 * own + reached - 1, 2 * own + reached + 1
                    )
        else:
            arrive(j + 1, lasts)
        finish(j)

    for j in order[:-2]:
        finish_after(j, due_relay, due_far)
    first_core = lax.rem(here, 2) == 0
    for turn, chosen in ((order[-2:], first_core), (order[:-3:-1], jnp.logical_not(first_core))):

        @pl.when(chosen)
        def _():
            relays, lasts = dict(due_relay), dict(due_far)
            for j in turn:
                finish_after(j, relays, lasts)

    for q in range(chunk):
        for source in range(peers):

            @pl.when(mem != source)
            def _():
                pltpu.make_async_remote_copy(
                    src_ref=terms.at[source * chunk + q],
                    dst_ref=terms_in.at[source, q],
                    send_sem=term_send.at[source * chunk + q],
                    recv_sem=term_recv.at[source, q],
                    device_id={"mem": jnp.int32(source)},
                    device_id_type=MESH,
                ).wait()

        result = terms_in[0, q]
        for source in range(1, peers):
            result = result + terms_in[source, q]
        out_ref[:, :, cols(q, q + 1)] = result
    for group_of in (lift_own, lift_relay, far_mid, far_last):
        for copy in group_of.values():
            copy.wait_send()
    far_two.wait_send()


def per_device(ens, control, col_count, level_index, pair_blocks, loc_blocks):
    own = col_count.shape[0]
    width = loc_blocks.shape[1]
    pairs = pair_blocks.shape[0]
    devices = lax.axis_size("grid")
    peers = lax.axis_size("mem")
    members, slots, levels, columns = ens.shape
    rows = members * levels
    extra = SPAN - own
    assert 0 < extra <= own and own % peers == 0 and devices > 2
    assert own % 2 == 0 and extra % 2 == 0 and pairs // own < 16

    chunk = own // peers
    sizes = (members, slots, levels, own, width, devices, peers)
    dma = pltpu.SemaphoreType.DMA
    operands = (col_count, level_index, pair_blocks.T, ens, control, loc_blocks)
    return pl.pallas_call(
        functools.partial(kernel, sizes),
        out_shape=jax.ShapeDtypeStruct((slots, levels, columns // peers), jnp.float32),
        in_specs=[pl.BlockSpec(memory_space=pltpu.HBM)] * 6,
        out_specs=pl.BlockSpec(memory_space=pltpu.VMEM),
        scratch_shapes=[
            pltpu.SMEM(col_count.shape, jnp.int32),
            pltpu.SMEM(level_index.shape, jnp.int32),
            pltpu.SMEM((2, pairs), jnp.int32),
            pltpu.SMEM((own * (SPAN + 1),), jnp.int32),
            pltpu.VMEM(ens.shape, ens.dtype),
            pltpu.VMEM(control.shape, control.dtype),
            pltpu.VMEM((pairs + 1, width, width), loc_blocks.dtype),
            pltpu.VMEM((own + SPAN, rows, width), jnp.bfloat16),
            pltpu.VMEM((SPAN, rows, width), jnp.bfloat16),
            pltpu.VMEM((extra, rows, width), jnp.bfloat16),
            pltpu.VMEM((own, rows, width), jnp.bfloat16),
            pltpu.VMEM((rows, columns), jnp.float32),
            pltpu.VMEM((own, slots, levels, width), jnp.float32),
            pltpu.VMEM((peers, chunk, slots, levels, width), jnp.float32),
            dma((3,)),
            dma,
            dma((2 * own,)),
            dma((SPAN,)),
            dma((SPAN,)),
            dma((SPAN,)),
            dma((SPAN,)),
            dma((own,)),
            dma((peers, chunk)),
        ],
        compiler_params=pltpu.CompilerParams(
            collective_id=0, has_side_effects=True, vmem_limit_bytes=32 * 1024 * 1024
        ),
        cost_estimate=pl.CostEstimate(
            flops=2 * rows * width * width * pairs * 2,
            bytes_accessed=ens.size * 2 + control.size * 4 + loc_blocks.size * 2,
            transcendentals=0,
        ),
    )(*[pltpu.with_memory_space_constraint(array, pltpu.HBM) for array in operands])


def solution(mesh):
    return jax.shard_map(
        per_device,
        mesh=mesh,
        in_specs=(
            P("mem", None, None, "grid"),
            P(None, None, "grid"),
            P("grid"),
            P(),
            P("grid", None),
            P("grid", None, None),
        ),
        out_specs=P(None, None, ("grid", "mem")),
        check_vma=False,
    )
```

```python
import functools

import jax
import jax.numpy as jnp
from jax import lax
from jax.experimental import pallas as pl
from jax.experimental.pallas import tpu as pltpu
from jax.sharding import PartitionSpec as P

SPAN = 12
MESH = pl.DeviceIdType.MESH


vertical_scale = 8.0


def pieces_of(own):
    extra = SPAN - own
    return [(first, 2) for first in (*range(own - extra, own, 2), *range(0, own - extra, 2))]


def messages_of(count):
    return [(first, 1) for first in range(count)]


def kernel(
    sizes,
    count_hbm,
    level_hbm,
    pair_hbm,
    ens_hbm,
    control_hbm,
    loc_hbm,
    out_ref,
    counts,
    level_at,
    listed,
    slot,
    ens,
    control,
    loc,
    table,
    far,
    relay_in,
    near_in,
    spread,
    terms,
    terms_in,
    small_sems,
    loc_sem,
    in_sems,
    lift_send,
    lift_recv,
    far_send,
    far_recv,
    term_send,
    term_recv,
):
    members, slots, levels, own, width, devices, peers = sizes
    extra = SPAN - own
    pairs = loc_hbm.shape[0]
    per_block = pairs // own
    here = lax.axis_index("grid")
    mem = lax.axis_index("mem")
    up = lax.rem(here + 1, devices)
    down = lax.rem(here + devices - 1, devices)
    pieces = pieces_of(own)

    def cols(first, last):
        return slice(first * width, last * width)

    small = [
        pltpu.make_async_copy(level_hbm, level_at, small_sems.at[0]),
        pltpu.make_async_copy(count_hbm, counts, small_sems.at[1]),
    ]
    load_pairs = pltpu.make_async_copy(pair_hbm, listed, small_sems.at[2])
    load_loc = pltpu.make_async_copy(loc_hbm, loc.at[pl.ds(0, pairs)], loc_sem)
    loads = {}
    for first, n in pieces:
        at = cols(first, first + n)
        loads[first] = (
            pltpu.make_async_copy(
                control_hbm.at[:, :, at], control.at[:, :, at], in_sems.at[2 * first]
            ),
            pltpu.make_async_copy(
                ens_hbm.at[:, :, :, at], ens.at[:, :, :, at], in_sems.at[2 * first + 1]
            ),
        )
    for copy in small:
        copy.start()
    for first, n in pieces[: extra // 2]:
        for copy in loads[first]:
            copy.start()

    barrier = pltpu.get_barrier_semaphore()
    for other in (up, down):
        pl.semaphore_signal(barrier, inc=1, device_id={"grid": other}, device_id_type=MESH)
    for away in range(1, peers):
        pl.semaphore_signal(
            barrier, inc=1, device_id={"mem": lax.rem(mem + away, peers)}, device_id_type=MESH
        )

    loc[pairs] = jnp.zeros((width, width), loc.dtype)

    group = max(g for g in range(1, members + 1) if members % g == 0 and g * levels <= 256)
    size = group * levels
    down_at = lax.broadcasted_iota(jnp.int32, (size, 1), 0)
    across_at = lax.broadcasted_iota(jnp.int32, (1, size), 1)
    level_down = jnp.zeros((size, 1), jnp.float32)
    level_across = jnp.zeros((1, size), jnp.float32)
    for copy in small:
        copy.wait()
    for l in range(levels):
        value = level_at[l].astype(jnp.float32)
        level_down = jnp.where(down_at % levels == l, value, level_down)
        level_across = jnp.where(across_at % levels == l, value, level_across)
    vert = jnp.exp(-jnp.abs(level_down - level_across) / vertical_scale)
    vert = jnp.where(down_at // levels == across_at // levels, vert, 0.0)

    lane = lax.broadcasted_iota(jnp.int32, (1, width), 1)

    def live(block):
        return (lane < counts[block]).astype(jnp.float32)

    def lift_copy(which, src, dst, n):
        return pltpu.make_async_remote_copy(
            src_ref=table.at[pl.ds(src, n)],
            dst_ref=table.at[pl.ds(dst, n)],
            send_sem=lift_send.at[which],
            recv_sem=lift_recv.at[which],
            device_id={"grid": down},
            device_id_type=MESH,
        )

    near_part = [(first, 2) for first in range(0, extra, 2)]
    far_part = [(first, 2) for first in range(extra, own, 2)]
    lift_own = {
        first: lift_copy(first, first, own + first, n) for first, n in near_part + far_part
    }
    lift_relay = {
        first: lift_copy(own + first, own + first, 2 * own + first, n)
        for first, n in messages_of(extra)
    }
    due = dict(lift_own)
    due_relay = dict(lift_relay)

    def arrive(last, waiting=due):
        for first in [f for f in waiting if f < last]:
            waiting.pop(first).wait_recv()

    def far_copy(which, src, dst_ref, n):
        return pltpu.make_async_remote_copy(
            src_ref=far.at[pl.ds(src, n)],
            dst_ref=dst_ref,
            send_sem=far_send.at[which],
            recv_sem=far_recv.at[which],
            device_id={"grid": up},
            device_id_type=MESH,
        )

    far_two = far_copy(own, own, relay_in, extra)
    far_mid = {
        first: far_copy(first, first, near_in.at[pl.ds(first, n)], n) for first, n in far_part
    }
    far_last = {
        first: far_copy(first, first, near_in.at[pl.ds(first, n)], n)
        for first, n in messages_of(extra)
    }
    due_far = dict(far_last)
    due_mid = dict(far_mid)

    def pair(i, k, least):
        return loc[slot[i * (SPAN + 1) + k] if least <= k <= SPAN else pairs]

    def blocks(first, last):
        return jnp.concatenate([table[b] for b in range(first, last)], axis=1)

    def from_below(j, n, first, last):
        stack = jnp.concatenate(
            [
                jnp.concatenate([pair(i, j + c - i, 1) for i in range(first, last)], axis=0)
                for c in range(n)
            ],
            axis=1,
        )
        return jnp.dot(blocks(first, last), stack, preferred_element_type=jnp.float32)

    def from_above(j, n, first, last):
        stack = jnp.concatenate(
            [
                jnp.concatenate([pair(j + c, s - j - c, 0) for s in range(first, last)], axis=1)
                for c in range(n)
            ],
            axis=0,
        )
        return lax.dot_general(
            blocks(first, last),
            stack,
            (((1,), (1,)), ((), ())),
            preferred_element_type=jnp.float32,
        )

    def lift(first, n):
        for copy in loads[first]:
            copy.wait()
        at = cols(first, first + n)
        mask = jnp.concatenate([live(first + c) for c in range(n)], axis=1)
        masked = [control[t, :, at] * mask for t in range(slots)]
        for g in range(members // group):
            weighted = []
            for m in range(g * group, (g + 1) * group):
                total = ens[m, 0, :, at].astype(jnp.float32) * masked[0]
                for t in range(1, slots):
                    total = total + ens[m, t, :, at].astype(jnp.float32) * masked[t]
                weighted.append(total)
            lifted = jnp.dot(
                vert,
                jnp.concatenate(weighted, axis=0),
                precision=lax.Precision.HIGHEST,
                preferred_element_type=jnp.float32,
            )
            for c in range(n):
                table[first + c, g * size : (g + 1) * size] = lifted[:, cols(c, c + 1)].astype(
                    table.dtype
                )

    def lift_and_send(first, n):
        lift(first, n)
        if first == pieces[0][0]:
            load_pairs.start()
            load_loc.start()
            for later, unused in pieces[extra // 2 :]:
                for copy in loads[later]:
                    copy.start()
            pl.semaphore_wait(barrier, 2 + peers - 1)
        lift_own[first].start()

    for first, n in pieces[: extra // 2]:
        lift_and_send(first, n)

    load_pairs.wait()
    low = 7
    for b in range(own):
        first_word = jnp.int32(0)
        second_word = jnp.int32(0)
        for p in range(per_block):
            k = listed[1, b * per_block + p] - listed[0, b * per_block + p]
            k = jnp.where(k < 0, k + own * devices, k)
            near = k < low
            code = jnp.int32(p + 1) << (4 * jnp.where(near, k, k - low))
            first_word = first_word + jnp.where(near, code, 0)
            second_word = second_word + jnp.where(near, 0, code)
        for k in range(SPAN + 1):
            word = first_word >> (4 * k) if k < low else second_word >> (4 * (k - low))
            place = word & 15
            at = jnp.minimum(b * per_block + place - 1, pairs)
            slot[b * (SPAN + 1) + k] = jnp.where(place == 0, pairs, at)

    load_loc.wait()

    def keep_far(at, total):
        for c in range(2):
            far[at + c] = total[:, cols(c, c + 1)].astype(far.dtype)

    for n in range(0, extra, 2):
        j = 2 * own + n
        keep_far(own + n, from_below(j, 2, j - SPAN, own))
    far_two.start()

    for first, n in pieces[extra // 2 :]:
        lift_and_send(first, n)

    for n in range(extra, own, 2):
        j = own + n
        keep_far(n, from_below(j, 2, j - SPAN, own))
        far_mid[n].start()

    first_core = lax.rem(here, 2) == 0

    def relay():
        waiting = dict(due)
        for first, n in messages_of(extra):
            arrive(first + n, waiting)
            lift_relay[first].start()

    pl.when(first_core)(relay)

    for n in range(0, extra, 2):
        j = own + n
        total = from_below(j, 2, max(0, j - SPAN), own)
        if n == 0:
            far_two.wait_recv()
        passing = jnp.concatenate([relay_in[n], relay_in[n + 1]], axis=1)
        keep_far(n, total + passing.astype(jnp.float32))
        for at in (n, n + 1):
            if at in far_last:
                far_last[at].start()

    for j in range(0, own, 2):
        spread[:, cols(j, j + 2)] = from_above(j, 2, j, own) + from_below(j, 2, 0, j + 1)

    pl.when(jnp.logical_not(first_core))(relay)
    for first in [f for f in due if f < extra]:
        due.pop(first)

    for first in range(0, own, 2):
        arrive(first + 2)
        source = own + first
        for j in range(0, own, 2):
            if source <= j + 1 + SPAN:
                spread[:, cols(j, j + 2)] += from_above(j, 2, source, source + 2)

    chunk = own // peers

    def finish(j):
        column = cols(j, j + 1)
        total = spread[:, column] + near_in[j].astype(jnp.float32)
        scale = live(j) / (members * peers - 1)
        for t in range(slots):
            mixed = ens[0, t, :, column].astype(jnp.float32) * total[:levels]
            for m in range(1, members):
                mixed = mixed + ens[m, t, :, column].astype(jnp.float32) * (
                    total[m * levels : (m + 1) * levels]
                )
            terms[j, t] = mixed * scale
        to = j // chunk

        @pl.when(mem != to)
        def _():
            pltpu.make_async_remote_copy(
                src_ref=terms.at[j],
                dst_ref=terms_in.at[mem, j % chunk],
                send_sem=term_send.at[j],
                recv_sem=term_recv.at[mem, j % chunk],
                device_id={"mem": jnp.int32(to)},
                device_id_type=MESH,
            ).start()

        @pl.when(mem == to)
        def _():
            terms_in[to, j % chunk] = terms[j]

    order = []
    for n in range(max(extra, own - extra)):
        order += [b for b in (extra + n, n) if extra <= b < own or b == n < extra]

    def finish_after(j, relays, lasts):
        if j >= extra:
            arrive(j + 1, due_mid)
            reached = j + SPAN - 2 * own
            arrive(reached + 1, relays)
            spread[:, cols(j, j + 1)] += from_above(
                j, 1, 2 * own + reached - reached % 2, 2 * own + reached + 1
            )
            if reached % 2 == 1:
                for later in range(j + 1, own):
                    spread[:, cols(later, later + 1)] += from_above(
                        later, 1, 2 * own + reached - 1, 2 * own + reached + 1
                    )
        else:
            arrive(j + 1, lasts)
        finish(j)

    for j in order[:-2]:
        finish_after(j, due_relay, due_far)
    for turn, chosen in ((order[-2:], first_core), (order[:-3:-1], jnp.logical_not(first_core))):

        @pl.when(chosen)
        def _():
            relays, lasts = dict(due_relay), dict(due_far)
            for j in turn:
                finish_after(j, relays, lasts)

    for q in range(chunk):
        for source in range(peers):

            @pl.when(mem != source)
            def _():
                pltpu.make_async_remote_copy(
                    src_ref=terms.at[source * chunk + q],
                    dst_ref=terms_in.at[source, q],
                    send_sem=term_send.at[source * chunk + q],
                    recv_sem=term_recv.at[source, q],
                    device_id={"mem": jnp.int32(source)},
                    device_id_type=MESH,
                ).wait()

        result = terms_in[0, q]
        for source in range(1, peers):
            result = result + terms_in[source, q]
        out_ref[:, :, cols(q, q + 1)] = result
    for group_of in (lift_own, lift_relay, far_mid, far_last):
        for copy in group_of.values():
            copy.wait_send()
    far_two.wait_send()


def per_device(ens, control, col_count, level_index, pair_blocks, loc_blocks):
    own = col_count.shape[0]
    width = loc_blocks.shape[1]
    pairs = pair_blocks.shape[0]
    devices = lax.axis_size("grid")
    peers = lax.axis_size("mem")
    members, slots, levels, columns = ens.shape
    rows = members * levels
    extra = SPAN - own
    assert 0 < extra <= own and own % peers == 0 and devices > 2
    assert own % 2 == 0 and extra % 2 == 0 and pairs // own < 16

    chunk = own // peers
    sizes = (members, slots, levels, own, width, devices, peers)
    dma = pltpu.SemaphoreType.DMA
    operands = (col_count, level_index, pair_blocks.T, ens, control, loc_blocks)
    return pl.pallas_call(
        functools.partial(kernel, sizes),
        out_shape=jax.ShapeDtypeStruct((slots, levels, columns // peers), jnp.float32),
        in_specs=[pl.BlockSpec(memory_space=pltpu.HBM)] * 6,
        out_specs=pl.BlockSpec(memory_space=pltpu.VMEM),
        scratch_shapes=[
            pltpu.SMEM(col_count.shape, jnp.int32),
            pltpu.SMEM(level_index.shape, jnp.int32),
            pltpu.SMEM((2, pairs), jnp.int32),
            pltpu.SMEM((own * (SPAN + 1),), jnp.int32),
            pltpu.VMEM(ens.shape, ens.dtype),
            pltpu.VMEM(control.shape, control.dtype),
            pltpu.VMEM((pairs + 1, width, width), loc_blocks.dtype),
            pltpu.VMEM((own + SPAN, rows, width), jnp.bfloat16),
            pltpu.VMEM((SPAN, rows, width), jnp.bfloat16),
            pltpu.VMEM((extra, rows, width), jnp.bfloat16),
            pltpu.VMEM((own, rows, width), jnp.bfloat16),
            pltpu.VMEM((rows, columns), jnp.float32),
            pltpu.VMEM((own, slots, levels, width), jnp.float32),
            pltpu.VMEM((peers, chunk, slots, levels, width), jnp.float32),
            dma((3,)),
            dma,
            dma((2 * own,)),
            dma((SPAN,)),
            dma((SPAN,)),
            dma((SPAN,)),
            dma((SPAN,)),
            dma((own,)),
            dma((peers, chunk)),
        ],
        compiler_params=pltpu.CompilerParams(
            collective_id=0, has_side_effects=True, vmem_limit_bytes=32 * 1024 * 1024
        ),
        cost_estimate=pl.CostEstimate(
            flops=2 * rows * width * width * pairs * 2,
            bytes_accessed=ens.size * 2 + control.size * 4 + loc_blocks.size * 2,
            transcendentals=0,
        ),
    )(*[pltpu.with_memory_space_constraint(array, pltpu.HBM) for array in operands])


def solution(mesh):
    return jax.shard_map(
        per_device,
        mesh=mesh,
        in_specs=(
            P("mem", None, None, "grid"),
            P(None, None, "grid"),
            P("grid"),
            P(),
            P("grid", None),
            P("grid", None, None),
        ),
        out_specs=P(None, None, ("grid", "mem")),
        check_vma=False,
    )
```
